32 devices in a mesh: row: 8 (over z, x), period: 4 (over y, core).
Axes of the slice: x: 2, y: 2, z: 4, core: 2. Of those that a mesh axis runs over, the one named last changes fastest.
Arguments:
- codes: int32 [2048, 64], P('row'), may hold values from 0 to 255
- node: int32 [2048], P('row'), may hold values from 0 to 15
- chosen: int32 [16, 32], replicated, may hold values from 0 to 63, all different within a row
- arm: int32 [2048], P('row'), may hold values 0 or 1
- honest: int32 [2048], P('row'), may hold values 0 or 1
- outcome: bfloat16 [2048, 128], P('row', 'period'), may hold values from -8 to 8
Outputs:
- gains: float32 [32, 16, 256], P('row', None, 'period')
- best_gain: float32 [16], replicated
- effect: float32 [16, 128], P(None, 'period')
The draws below stay inside these ranges and needn't reach their ends.
Inputs may be any that keep to these rules, and one draw needn't show every extreme that they name: Each row of chosen holds 32 different covariate ids.
All inputs are finite; a program needn't handle non-finite values. No bound on the sum of `arm` or of `honest` on one device may be relied on, other than what follows from the above.
Results may differ from the reference program's by a relative error of at most 0.001.
Values may be sent and summed in bfloat16 or wider, within the bound.
No kernel may reach another device: no remote copies, remote signals or barrier semaphores. Data moves between devices by JAX's collectives and lax.ppermute only.
A program may use at most 128 MiB of HBM per device.

```python
import jax
import jax.numpy as jnp
from jax import lax

NODES = 16
SLOTS = 32
COVARS = 64
BINS = 256
WEEKS = 128
ROWS = 2048


def draw_outcome(key, part):
    key_base = jax.random.fold_in(key, 0)
    base = jax.random.normal(key_base, (ROWS, WEEKS), jnp.float32)
    position = jnp.arange(ROWS, dtype=jnp.float32) / ROWS
    row_scale = 0.5 * jnp.exp(jnp.log(3.0) * position)
    values = row_scale[:, None] * jnp.clip(base, -4.0, 4.0)
    return jnp.clip(values, -8.0, 8.0).astype(jnp.bfloat16)


def with_ends(array, key, low, largest):
    longest = array.shape.index(max(array.shape))
    spots = []
    for shift in (0, 1):
        where = [jax.random.randint(jax.random.fold_in(key, axis), (), 0, length) for axis, length in enumerate(array.shape)]
        where[longest] = (where[longest] + shift) % array.shape[longest]
        spots.append(tuple(where))
    return array.at[spots[0]].set(low).at[spots[1]].set(largest)


def choose_distinct(own_key, rows, number_of, top, lift):
    ranking = jax.random.permutation(jax.random.fold_in(own_key, 1), number_of)
    favour = ranking
    for power in range(3):
        favour = favour * favour // number_of
    favour = favour * lift // number_of
    lots = jax.random.randint(jax.random.fold_in(own_key, 2), (rows, number_of), 0, 4096) + favour
    holders = jax.random.permutation(jax.random.fold_in(own_key, 3), rows)[jnp.arange(number_of) % rows]
    lots = jnp.where(jnp.arange(rows)[:, None] == holders[None, :], 1 << 14, lots)
    priority = lots * number_of + jnp.arange(number_of)
    return lax.top_k(priority.astype(jnp.int32), top)[1].astype(jnp.int32)


def setup_inputs(seed: int = 0) -> dict:
    seeds = jax.random.split(jax.random.key(seed), 7)
    return {
        "codes": with_ends(jax.random.randint(seeds[0], (ROWS, COVARS), 0, BINS), jax.random.fold_in(seeds[0], 1), 0, BINS - 1).astype(jnp.int32),
        "node": with_ends(jax.random.randint(seeds[1], (ROWS,), 0, NODES), jax.random.fold_in(seeds[1], 1), 0, NODES - 1).astype(jnp.int32),
        "chosen": choose_distinct(seeds[2], NODES, COVARS, SLOTS, 0),
        "arm": with_ends((jax.random.randint(seeds[3], (ROWS,), 0, 2) < 1).astype(jnp.int32), jax.random.fold_in(seeds[3], 1), 0, 1),
        "honest": with_ends((jax.random.randint(seeds[4], (ROWS,), 0, 2) < 1).astype(jnp.int32), jax.random.fold_in(seeds[4], 1), 0, 1),
        "outcome": draw_outcome(jax.random.fold_in(seeds[6], 71), 0),
    }


def split_gain(left_sums, right_sums, weeks):
    def effect_of(sums):
        treated = sums[..., :weeks] / (sums[..., 2 * weeks:2 * weeks + 1] + 1.0)
        control = sums[..., weeks:2 * weeks] / (sums[..., 2 * weeks + 1:2 * weeks + 2] + 1.0)
        return treated - control

    spread_gap = effect_of(left_sums) - effect_of(right_sums)
    left_n = left_sums[..., 2 * weeks] + left_sums[..., 2 * weeks + 1]
    right_n = right_sums[..., 2 * weeks] + right_sums[..., 2 * weeks + 1]
    balance = left_n * right_n / ((left_n + right_n + 1.0) * (left_n + right_n + 1.0))
    return balance * jnp.sum(spread_gap * spread_gap, axis=-1)


def reference(codes, node, chosen, arm, honest, outcome):
    outcome_f = outcome.astype(jnp.float32)
    arm_f = arm.astype(jnp.float32)
    honest_f = honest.astype(jnp.float32)
    treated = honest_f * arm_f
    control = honest_f * (1.0 - arm_f)
    stat_cols = jnp.concatenate([outcome_f * treated[:, None], outcome_f * control[:, None], treated[:, None], control[:, None]], axis=1)
    picked = jnp.take_along_axis(codes, chosen[node], axis=1)
    row_keys = (node[:, None] * BINS + picked).astype(jnp.int32)

    def histogram(column):
        return jax.ops.segment_sum(stat_cols, column, num_segments=NODES * BINS)

    hist = lax.map(histogram, row_keys.T)
    hist = hist.reshape(SLOTS, NODES, BINS, 2 * WEEKS + 2)
    left_sums = jnp.cumsum(hist, axis=2)
    right_sums = left_sums[:, :, -1:, :] - left_sums
    gains = split_gain(left_sums, right_sums, WEEKS)
    best_gain = jnp.max(gains, axis=(0, 2))
    kept = 1.0 - honest_f
    node_hot = (node[:, None] == jnp.arange(NODES, dtype=jnp.int32)[None, :]).astype(jnp.float32)
    est_cols = jnp.concatenate([outcome_f * (kept * arm_f)[:, None], outcome_f * (kept * (1.0 - arm_f))[:, None]], axis=1)
    est_sums = jnp.dot(node_hot.T, est_cols, precision=lax.Precision.HIGHEST)
    est_counts = jnp.dot(node_hot.T, jnp.stack([kept * arm_f, kept * (1.0 - arm_f)], axis=1), precision=lax.Precision.HIGHEST)
    effect = est_sums[:, :WEEKS] / (est_counts[:, 0:1] + 1.0) - est_sums[:, WEEKS:] / (est_counts[:, 1:2] + 1.0)
    return gains, best_gain, effect
```

```python
import functools

import jax
import jax.numpy as jnp
from jax import lax
from jax.experimental import pallas as pl
from jax.experimental.pallas import tpu as pltpu
from jax.sharding import PartitionSpec as P

NODES = 16
BINS = 256
LANES = 128
PAIRS = NODES // 2
BF16 = jnp.bfloat16
F32 = jnp.float32
NT = (((1,), (1,)), ((), ()))


def iota(shape, axis):
    return lax.broadcasted_iota(jnp.int32, shape, axis)


def dot(a, b, dims=(((1,), (0,)), ((), ()))):
    return lax.dot_general(a.astype(BF16), b.astype(BF16), dims, preferred_element_type=F32)


def block_rows(weeks, per_owner):
    return -(-(weeks + 8 + per_owner) // 16) * 16


def pack_kernel(owners, codes_ref, node_ref, arm_ref, honest_ref, chosen_ref, outcome_ref, own_ref, away_ref, scratch):
    units, covars = codes_ref.shape
    slots, weeks = chosen_ref.shape[1], outcome_ref.shape[1]
    per_owner = slots // owners
    rows = own_ref.shape[0] - slots // 2
    room = units // PAIRS
    me = lax.axis_index("row")
    node, arm, honest = node_ref[...], arm_ref[...], honest_ref[...]

    before = (iota((units, units), 0) < iota((units, units), 1)).astype(BF16)
    pair = lax.shift_right_logical(node, 1)
    group = iota((PAIRS, units), 0)
    in_pair = ((group == pair) & (honest == 1)).astype(F32)
    held = jnp.minimum(jnp.sum(in_pair, axis=1, keepdims=True), float(room))
    index = jnp.sum(in_pair * dot(in_pair, before), axis=0, keepdims=True)
    placed = (honest == 1) & (index < room)
    filler = jnp.broadcast_to(jnp.where(placed, 0.0, 1.0), (8, units))
    filler_rank = dot(filler, before)[0:1]
    free = jnp.broadcast_to(room - held, (PAIRS, units))
    lower = (iota((PAIRS, PAIRS), 1) < iota((PAIRS, PAIRS), 0)).astype(BF16)
    first = dot(lower, free)
    in_gap = (filler_rank >= first) & (filler_rank < first + free)
    gap_lane = jnp.sum(
        jnp.where(in_gap, group.astype(F32) * room + held - first + filler_rank, 0.0), axis=0, keepdims=True
    )
    lane = jnp.where(placed, pair * room + index.astype(jnp.int32), gap_lane.astype(jnp.int32))
    lane = lane ^ (room * (me & 3))
    place = jnp.where(iota((units, units), 0) == lane, 1.0, 0.0).astype(BF16)

    keys = jnp.concatenate(
        [node.astype(F32), arm.astype(F32), honest.astype(F32), jnp.zeros((5, units), F32)], axis=0
    )
    wide = jnp.concatenate(
        [outcome_ref[...].astype(F32), codes_ref[...].astype(F32), jnp.zeros((units, LANES - weeks - covars), F32)], axis=1
    )
    sorted_wide = dot(jnp.concatenate([wide.T, keys], axis=0), place, NT)
    sorted_keys = sorted_wide[LANES:]

    flat = jnp.concatenate([chosen_ref[n : n + 1, :] for n in range(NODES)], axis=1)
    hot = jnp.where(iota((covars, NODES * slots), 0) == flat, 1.0, 0.0)
    per_node = dot(hot, sorted_wide[weeks : weeks + covars], (((0,), (0,)), ((), ())))
    picked = jnp.zeros((slots, units), F32)
    for n in range(NODES):
        picked = picked + jnp.where(sorted_keys[0:1] == float(n), per_node[n * slots : (n + 1) * slots], 0.0)
    for j in range(owners):
        scratch[j, 0:per_owner] = picked[j * per_owner : (j + 1) * per_owner]

    common = jnp.concatenate(
        [sorted_wide[0:weeks], sorted_keys, jnp.zeros((rows - weeks - 8, units), F32)], axis=0
    ).astype(BF16)
    half = owners // 2
    for start, out in ((0, own_ref), (half, away_ref)):
        mine = jnp.concatenate([scratch[me ^ (start + j)][0:per_owner] for j in range(half)], axis=0)
        out[0:rows] = common
        out[rows:] = mine.astype(BF16)


def gain_kernel(layout, weeks, per_owner, *refs):
    n_in = len(layout)
    blocks = refs[:n_in]
    gain_ref, effect_ref, sums, steps, outs, keys = refs[n_in:]
    depth = outs.shape[2]
    me = lax.axis_index("row")
    where_of = {}
    for ref, (ids, pick_row) in zip(blocks, layout):
        for at, k in enumerate(ids):
            where_of[k] = (ref, at, pick_row)
    n_blocks = len(where_of)
    quarter = lax.shift_right_logical(iota((8, LANES), 1), 5) ^ (me & 3)
    masks = [quarter == t for t in range(4)]
    bins_up = (iota((BINS, depth), 0) + 1).astype(F32).astype(BF16)
    one, zero = jnp.ones((), BF16), jnp.zeros((), BF16)

    def loaded(k, half):
        ref, at, pick_row = where_of[k]
        lanes = slice(half * LANES, (half + 1) * LANES)
        body = ref[at, 0 : weeks + 16, lanes].astype(F32)
        if pick_row == weeks + 8:
            return body
        picks = ref[at, pick_row : pick_row + per_owner, lanes].astype(F32)
        return jnp.concatenate([body[0 : weeks + 8], picks, jnp.zeros((8 - per_owner, LANES), F32)], axis=0)

    def week_rows(g, out, key):
        node, arm, honest = key[0:1], key[1:2], key[2:3]
        rows, counts = [], []
        for m in range(2):
            mine = (node == (2 * g + m).astype(F32)) & (honest == 1.0)
            for a in (1.0, 0.0):
                here = jnp.where(mine & (arm == a), 1.0, 0.0)
                rows.append(out * here)
                counts.append(here)
        counts.append(jnp.zeros((12, out.shape[1]), F32))
        return jnp.concatenate(rows + counts, axis=0).astype(BF16)

    strays = jnp.zeros((1, depth), F32)
    est = jnp.zeros((2 * NODES, weeks), F32)
    est_units = jnp.zeros((2 * NODES, depth), F32)
    for half in range(2):
        held = [loaded(k, half) for k in range(n_blocks)]
        for g in range(half * 4, half * 4 + 4):
            parts = []
            for first in range(0, n_blocks, 4):
                part = held[first]
                for k in range(first + 1, first + 4):
                    mask = jnp.concatenate([masks[(g ^ k) & 3]] * (part.shape[0] // 8), axis=0)
                    part = jnp.where(mask, held[k], part)
                parts.append(part)
            block = jnp.concatenate(parts, axis=1)
            out, key, picks = block[0:weeks], block[weeks : weeks + 8], block[weeks + 8 : weeks + 8 + per_owner]
            outs[g] = out
            keys[g] = key
            node, arm, honest = key[0:1], key[1:2], key[2:3]
            strays = strays + jnp.where((honest == 1.0) & ((node < 2.0 * g) | (node > 2.0 * g + 1.0)), 1.0, 0.0)
            kept = jnp.where(honest == 0.0, node, -1.0)
            kept_hot = kept == iota((NODES, depth), 0).astype(F32)
            hot = jnp.concatenate(
                [jnp.where(kept_hot & (arm == a), 1.0, 0.0) for a in (1.0, 0.0)], axis=0
            )
            est = est + dot(hot, out, NT)
            est_units = est_units + hot
            for s in range(per_owner):
                pick = jnp.broadcast_to(picks[s : s + 1], (16, depth)).astype(BF16)
                pick = jnp.concatenate([pick] * (BINS // 16), axis=0)
                steps[g, s * BINS : (s + 1) * BINS] = jnp.maximum(jnp.minimum(bins_up - pick, one), zero)
            sums[g] = dot(week_rows(jnp.int32(g), out, key), steps[g], NT)

    units = jnp.sum(est_units, axis=1, keepdims=True)
    effect_ref[...] = est[0:NODES] / (units[0:NODES] + 1.0) - est[NODES:] / (units[NODES:] + 1.0)

    @pl.when(jnp.sum(strays) > 0.0)
    def _():
        def over(i, carry):
            g, other = i // PAIRS, i % PAIRS

            @pl.when(g != other)
            def _():
                sums[g] += dot(week_rows(g, outs[other], keys[other]), steps[other], NT)

            return carry

        lax.fori_loop(0, PAIRS * PAIRS, over, 0)

    for g in range(PAIRS):
        for m in range(2):
            base = 2 * m * weeks
            treated, control = sums[g, base : base + weeks], sums[g, base + weeks : base + 2 * weeks]
            counts = sums[g, 4 * weeks + 2 * m : 4 * weeks + 2 * m + 2]
            lt, lc = counts[0:1], counts[1:2]
            last = slice(BINS - 1, BINS)
            rt, rc = lt[:, last] - lt, lc[:, last] - lc
            it, ic = 1.0 / (rt + 1.0), 1.0 / (rc + 1.0)
            gap = (
                treated * (1.0 / (lt + 1.0) + it)
                - control * (1.0 / (lc + 1.0) + ic)
                - (treated[:, last] * it - control[:, last] * ic)
            )
            cl, cr = lt + lc, rt + rc
            balance = cl * cr / ((cl + cr + 1.0) * (cl + cr + 1.0))
            gain_ref[2 * g + m : 2 * g + m + 1] = balance * jnp.sum(gap * gap, axis=0, keepdims=True)


def finish_kernel(a_ref, b_ref, gain_ref, best_ref):
    per_owner, _, share = gain_ref.shape
    at = lax.axis_index("period") * share
    total = a_ref[...] + b_ref[...]
    best = jnp.broadcast_to(jnp.max(total, axis=1, keepdims=True), (NODES, LANES))
    best_ref[...] = best.T[0:1, 0:NODES]
    for s in range(per_owner):
        turned = pltpu.roll(total[:, s * BINS : (s + 1) * BINS], BINS - at, 1)
        gain_ref[s] = turned[:, 0:share]


def shards(codes, node, chosen, arm, honest, outcome):
    units, weeks = outcome.shape
    slots = chosen.shape[1]
    owners, periods = lax.axis_size("row"), lax.axis_size("period")
    per_owner = slots // owners
    rows = block_rows(weeks, per_owner)
    vmem = pl.BlockSpec(memory_space=pltpu.VMEM)

    def swap(x, axis, bit):
        return lax.ppermute(x, axis, [(i, i ^ bit) for i in range(lax.axis_size(axis))])

    packed = jax.ShapeDtypeStruct((rows + slots // 2, units), BF16)
    own, away = pl.pallas_call(
        functools.partial(pack_kernel, owners),
        out_shape=(packed, packed),
        in_specs=[vmem] * 6,
        out_specs=(vmem, vmem),
        scratch_shapes=[pltpu.VMEM((owners, -(-per_owner // 8) * 8, units), F32)],
    )(codes, node.reshape(1, units), arm.reshape(1, units), honest.reshape(1, units), chosen, outcome)

    groups, bit = owners // 2, owners // 2
    held = [(own[None], [0]), (swap(away, "row", bit)[None], [bit])]
    while groups > 4:
        groups, bit = groups // 2, bit // 2
        cut = rows + groups * per_owner
        ids = [k for _, part in held for k in part]
        send = jnp.concatenate([jnp.concatenate([x[:, :rows], x[:, cut:]], axis=1) for x, _ in held], axis=0)
        keep = jnp.concatenate([x[:, :cut] for x, _ in held], axis=0)
        held = [(keep, ids), (swap(send, "row", bit), [k ^ bit for k in ids])]
    ids = [k for _, part in held for k in part]
    layout = [(part, rows) for _, part in held]
    blocks = [x for x, _ in held]
    for k in (3, 2, 1):
        send = jnp.concatenate(
            [
                jnp.concatenate(
                    [
                        x[:, : weeks + 8],
                        x[:, rows + k * per_owner : rows + (k + 1) * per_owner],
                        x[:, weeks + 8 + per_owner : rows],
                    ],
                    axis=1,
                )
                for x, _ in held
            ],
            axis=0,
        )
        blocks.append(swap(send, "row", k))
        layout.append(([i ^ k for i in ids], weeks + 8))

    depth = owners * units // PAIRS
    wide = per_owner * BINS
    gain, effect = pl.pallas_call(
        functools.partial(gain_kernel, layout, weeks, per_owner),
        out_shape=(jax.ShapeDtypeStruct((NODES, wide), F32), jax.ShapeDtypeStruct((NODES, weeks), F32)),
        in_specs=[vmem] * len(blocks),
        out_specs=(vmem, vmem),
        scratch_shapes=[
            pltpu.VMEM((PAIRS, 4 * weeks + 16, wide), F32),
            pltpu.VMEM((PAIRS, wide, depth), BF16),
            pltpu.VMEM((PAIRS, weeks, depth), F32),
            pltpu.VMEM((PAIRS, 8, depth), F32),
        ],
        compiler_params=pltpu.CompilerParams(vmem_limit_bytes=40 * 1024 * 1024),
    )(*blocks)

    bit = 1
    while 2 * bit < periods:
        gain = gain + swap(gain, "period", bit)
        bit *= 2
    gains, best = pl.pallas_call(
        finish_kernel,
        out_shape=(
            jax.ShapeDtypeStruct((per_owner, NODES, BINS // periods), F32),
            jax.ShapeDtypeStruct((1, NODES), F32),
        ),
        in_specs=[vmem, vmem],
        out_specs=(vmem, vmem),
    )(gain, swap(gain, "period", bit))
    bit = 1
    while bit < owners:
        best = jnp.maximum(best, swap(best, "row", bit))
        bit *= 2
    return gains, best.reshape(NODES), effect


def solution(mesh):
    in_specs = (P("row", None), P("row"), P(), P("row"), P("row"), P("row", "period"))
    out_specs = (P("row", None, "period"), P(), P(None, "period"))
    return jax.shard_map(shards, mesh=mesh, in_specs=in_specs, out_specs=out_specs, check_vma=False)
```

```python
import functools

import jax
import jax.numpy as jnp
from jax import lax
from jax.experimental import pallas as pl
from jax.experimental.pallas import tpu as pltpu
from jax.sharding import PartitionSpec as P

NODES = 16
BINS = 256
LANES = 128
PAIRS = NODES // 2
BF16 = jnp.bfloat16
F32 = jnp.float32
NT = (((1,), (1,)), ((), ()))


def iota(shape, axis):
    return lax.broadcasted_iota(jnp.int32, shape, axis)


def dot(a, b, dims=(((1,), (0,)), ((), ()))):
    return lax.dot_general(a.astype(BF16), b.astype(BF16), dims, preferred_element_type=F32)


def block_rows(weeks, per_owner):
    return weeks + -(-(4 + per_owner) // 8) * 8


def pack_kernel(owners, codes_ref, node_ref, arm_ref, honest_ref, chosen_ref, outcome_ref, own_ref, away_ref, scratch):
    covars, units = codes_ref.shape
    slots, weeks = chosen_ref.shape[1], outcome_ref.shape[0]
    per_owner = slots // owners
    rows = own_ref.shape[0] - slots // 2
    room = units // PAIRS
    me = lax.axis_index("row")
    node, arm, honest = node_ref[...], arm_ref[...], honest_ref[...]

    before = (iota((units, units), 0) < iota((units, units), 1)).astype(BF16)
    pair = lax.shift_right_logical(node, 1)
    group = iota((PAIRS, units), 0)
    in_pair = ((group == pair) & (honest == 1)).astype(F32)
    held = jnp.minimum(jnp.sum(in_pair, axis=1, keepdims=True), float(room))
    index = jnp.sum(in_pair * dot(in_pair, before), axis=0, keepdims=True)
    placed = (honest == 1) & (index < room)
    filler = jnp.broadcast_to(jnp.where(placed, 0.0, 1.0), (8, units))
    filler_rank = dot(filler, before)[0:1]
    free = jnp.broadcast_to(room - held, (PAIRS, units))
    lower = (iota((PAIRS, PAIRS), 1) < iota((PAIRS, PAIRS), 0)).astype(BF16)
    first = dot(lower, free)
    in_gap = (filler_rank >= first) & (filler_rank < first + free)
    gap_lane = jnp.sum(
        jnp.where(in_gap, group.astype(F32) * room + held - first + filler_rank, 0.0), axis=0, keepdims=True
    )
    lane = jnp.where(placed, pair * room + index.astype(jnp.int32), gap_lane.astype(jnp.int32))
    lane = lane ^ (room * (me & 3))
    place = jnp.where(iota((units, units), 0) == lane, 1.0, 0.0).astype(BF16)

    keys = jnp.concatenate(
        [node.astype(F32), arm.astype(F32), honest.astype(F32), jnp.zeros((5, units), F32)], axis=0
    )
    wide = jnp.concatenate([outcome_ref[...].astype(F32), codes_ref[...].astype(F32), keys], axis=0)
    sorted_wide = dot(wide, place, NT)
    sorted_keys = sorted_wide[weeks + covars :]

    flat = jnp.concatenate([chosen_ref[n : n + 1, :] for n in range(NODES)], axis=1)
    hot = jnp.where(iota((covars, NODES * slots), 0) == flat, 1.0, 0.0)
    per_node = dot(hot, sorted_wide[weeks : weeks + covars], (((0,), (0,)), ((), ())))
    picked = jnp.zeros((slots, units), F32)
    for n in range(NODES):
        picked = picked + jnp.where(sorted_keys[0:1] == float(n), per_node[n * slots : (n + 1) * slots], 0.0)
    for j in range(owners):
        scratch[j, 0:per_owner] = picked[j * per_owner : (j + 1) * per_owner]

    half = owners // 2
    assert rows == weeks + 8
    for start, out in ((0, own_ref), (half, away_ref)):
        mine = [scratch[me ^ (start + j)][0:per_owner] for j in range(half)]
        out[0:rows] = jnp.concatenate(
            [sorted_wide[0:weeks], sorted_keys[0:4], mine[0], sorted_keys[4 + per_owner :]][: 3 + (per_owner < 4)], axis=0
        ).astype(BF16)
        out[rows:] = jnp.concatenate(mine, axis=0).astype(BF16)


def gain_kernel(layout, weeks, per_owner, *refs):
    n_in = len(layout)
    blocks = refs[:n_in]
    gain_ref, effect_ref, sums, steps, outs, keys = refs[n_in:]
    depth = outs.shape[2]
    me = lax.axis_index("row")
    where_of = {k: (ref, at) for ref, ids in zip(blocks, layout) for at, k in enumerate(ids)}
    n_blocks = len(where_of)
    rows = block_rows(weeks, per_owner)
    quarter = lax.shift_right_logical(iota((8, LANES), 1), 5) ^ (me & 3)
    masks = [quarter == t for t in range(4)]
    bins_up = (iota((BINS, depth), 0) + 1).astype(F32).astype(BF16)
    one, zero = jnp.ones((), BF16), jnp.zeros((), BF16)

    def loaded(k, half):
        ref, at = where_of[k]
        return ref[at, 0:rows, half * LANES : (half + 1) * LANES].astype(F32)

    def week_rows(g, out, key):
        node, arm, honest = key[0:1], key[1:2], key[2:3]
        rows, counts = [], []
        for m in range(2):
            mine = (node == (2 * g + m).astype(F32)) & (honest == 1.0)
            for a in (1.0, 0.0):
                here = jnp.where(mine & (arm == a), 1.0, 0.0)
                rows.append(out * here)
                counts.append(here)
        counts.append(jnp.zeros((12, out.shape[1]), F32))
        return jnp.concatenate(rows + counts, axis=0).astype(BF16)

    strays = jnp.zeros((1, depth), F32)
    est = jnp.zeros((2 * NODES, weeks), F32)
    est_units = jnp.zeros((2 * NODES, depth), F32)
    for half in range(2):
        held = [loaded(k, half) for k in range(n_blocks)]
        for g in range(half * 4, half * 4 + 4):
            parts = []
            for first in range(0, n_blocks, 4):
                part = held[first]
                for k in range(first + 1, first + 4):
                    mask = jnp.concatenate([masks[(g ^ k) & 3]] * (part.shape[0] // 8), axis=0)
                    part = jnp.where(mask, held[k], part)
                parts.append(part)
            block = jnp.concatenate(parts, axis=1)
            out, key, picks = block[0:weeks], block[weeks : weeks + 8], block[weeks + 4 : weeks + 4 + per_owner]
            outs[g] = out
            keys[g] = key
            node, arm, honest = key[0:1], key[1:2], key[2:3]
            strays = strays + jnp.where((honest == 1.0) & ((node < 2.0 * g) | (node > 2.0 * g + 1.0)), 1.0, 0.0)
            kept = jnp.where(honest == 0.0, node, -1.0)
            kept_hot = kept == iota((NODES, depth), 0).astype(F32)
            hot = jnp.concatenate(
                [jnp.where(kept_hot & (arm == a), 1.0, 0.0) for a in (1.0, 0.0)], axis=0
            )
            est = est + dot(hot, out, NT)
            est_units = est_units + hot
            for s in range(per_owner):
                pick = jnp.broadcast_to(picks[s : s + 1], (16, depth)).astype(BF16)
                pick = jnp.concatenate([pick] * (BINS // 16), axis=0)
                steps[g, s * BINS : (s + 1) * BINS] = jnp.maximum(jnp.minimum(bins_up - pick, one), zero)
            sums[g] = dot(week_rows(jnp.int32(g), out, key), steps[g], NT)

    units = jnp.sum(est_units, axis=1, keepdims=True)
    effect_ref[...] = est[0:NODES] / (units[0:NODES] + 1.0) - est[NODES:] / (units[NODES:] + 1.0)

    @pl.when(jnp.sum(strays) > 0.0)
    def _():
        def over(i, carry):
            g, other = i // PAIRS, i % PAIRS

            @pl.when(g != other)
            def _():
                sums[g] += dot(week_rows(g, outs[other], keys[other]), steps[other], NT)

            return carry

        lax.fori_loop(0, PAIRS * PAIRS, over, 0)

    for g in range(PAIRS):
        for m in range(2):
            base = 2 * m * weeks
            treated, control = sums[g, base : base + weeks], sums[g, base + weeks : base + 2 * weeks]
            counts = sums[g, 4 * weeks + 2 * m : 4 * weeks + 2 * m + 2]
            lt, lc = counts[0:1], counts[1:2]
            last = slice(BINS - 1, BINS)
            rt, rc = lt[:, last] - lt, lc[:, last] - lc
            it, ic = 1.0 / (rt + 1.0), 1.0 / (rc + 1.0)
            gap = (
                treated * (1.0 / (lt + 1.0) + it)
                - control * (1.0 / (lc + 1.0) + ic)
                - (treated[:, last] * it - control[:, last] * ic)
            )
            cl, cr = lt + lc, rt + rc
            balance = cl * cr / ((cl + cr + 1.0) * (cl + cr + 1.0))
            gain = balance * jnp.sum(gap * gap, axis=0, keepdims=True)
            for s in range(per_owner):
                gain_ref[s, 2 * g + m : 2 * g + m + 1] = gain[:, s * BINS : (s + 1) * BINS]


def shards(codes, node, chosen, arm, honest, outcome):
    units, weeks = outcome.shape
    slots = chosen.shape[1]
    owners, periods = lax.axis_size("row"), lax.axis_size("period")
    per_owner = slots // owners
    rows = block_rows(weeks, per_owner)
    vmem = pl.BlockSpec(memory_space=pltpu.VMEM)

    def swap(x, axis, bit):
        return lax.ppermute(x, axis, [(i, i ^ bit) for i in range(lax.axis_size(axis))])

    packed = jax.ShapeDtypeStruct((rows + slots // 2, units), BF16)
    own, away = pl.pallas_call(
        functools.partial(pack_kernel, owners),
        out_shape=(packed, packed),
        in_specs=[vmem] * 6,
        out_specs=(vmem, vmem),
        scratch_shapes=[pltpu.VMEM((owners, -(-per_owner // 8) * 8, units), F32)],
    )(codes.T, node.reshape(1, units), arm.reshape(1, units), honest.reshape(1, units), chosen, outcome.T)

    def part(x, first, last):
        bins = x[:, rows + first * per_owner : rows + last * per_owner]
        block = [x[:, : weeks + 4], bins[:, :per_owner], x[:, weeks + 4 + per_owner : rows]]
        return jnp.concatenate(block + ([bins] if last > first + 1 else []), axis=1)

    groups, bit = owners // 2, owners // 2
    held = [(own[None], [0]), (swap(away, "row", bit)[None], [bit])]
    while groups > 4:
        groups, bit = groups // 2, bit // 2
        ids = [k for _, some in held for k in some]
        send = jnp.concatenate([part(x, groups, 2 * groups) for x, _ in held], axis=0)
        keep = jnp.concatenate([x[:, : rows + groups * per_owner] for x, _ in held], axis=0)
        held = [(keep, ids), (swap(send, "row", bit), [k ^ bit for k in ids])]
    ids = [k for _, some in held for k in some]
    layout = [some for _, some in held]
    blocks = [x for x, _ in held]
    for k in (3, 2, 1):
        send = jnp.concatenate([part(x, k, k + 1) for x, _ in held], axis=0)
        blocks.append(swap(send, "row", k))
        layout.append([i ^ k for i in ids])

    depth = owners * units // PAIRS
    wide = per_owner * BINS
    gain, effect = pl.pallas_call(
        functools.partial(gain_kernel, layout, weeks, per_owner),
        out_shape=(jax.ShapeDtypeStruct((per_owner, NODES, BINS), F32), jax.ShapeDtypeStruct((NODES, weeks), F32)),
        in_specs=[vmem] * len(blocks),
        out_specs=(vmem, vmem),
        scratch_shapes=[
            pltpu.VMEM((PAIRS, 4 * weeks + 16, wide), F32),
            pltpu.VMEM((PAIRS, wide, depth), BF16),
            pltpu.VMEM((PAIRS, weeks, depth), F32),
            pltpu.VMEM((PAIRS, 8, depth), F32),
        ],
        compiler_params=pltpu.CompilerParams(vmem_limit_bytes=40 * 1024 * 1024),
    )(*blocks)

    gain = gain + swap(gain, "period", 1)
    bit = 2
    while bit < periods:
        gain = gain + swap(gain, "period", bit | 1)
        bit *= 2
    share = BINS // periods
    gains = lax.dynamic_slice_in_dim(gain, lax.axis_index("period") * share, share, 2)
    best = jnp.max(gain, axis=(0, 2))
    bit = 1
    while bit < owners:
        best = jnp.maximum(best, swap(best, ("row", "period"), bit * periods | 1))
        bit *= 2
    return gains, best, effect


def solution(mesh):
    in_specs = (P("row", None), P("row"), P(), P("row"), P("row"), P("row", "period"))
    out_specs = (P("row", None, "period"), P(), P(None, "period"))
    return jax.shard_map(shards, mesh=mesh, in_specs=in_specs, out_specs=out_specs, check_vma=False)
```

```python
import functools

import jax
import jax.numpy as jnp
from jax import lax
from jax.experimental import pallas as pl
from jax.experimental.pallas import tpu as pltpu
from jax.sharding import PartitionSpec as P

NODES = 16
BINS = 256
LANES = 128
PAIRS = NODES // 2
BF16 = jnp.bfloat16
F32 = jnp.float32
NT = (((1,), (1,)), ((), ()))


def iota(shape, axis):
    return lax.broadcasted_iota(jnp.int32, shape, axis)


def dot(a, b, dims=(((1,), (0,)), ((), ()))):
    return lax.dot_general(a.astype(BF16), b.astype(BF16), dims, preferred_element_type=F32)


def block_rows(weeks, per_owner):
    return weeks + -(-(4 + per_owner) // 8) * 8


def pack_kernel(owners, codes_ref, node_ref, arm_ref, honest_ref, chosen_ref, outcome_ref, own_ref, away_ref, scratch):
    covars, units = codes_ref.shape
    slots, weeks = chosen_ref.shape[1], outcome_ref.shape[0]
    per_owner = slots // owners
    rows = own_ref.shape[0] - slots // 2
    room = units // PAIRS
    me = lax.axis_index("row")
    node, arm, honest = node_ref[...], arm_ref[...], honest_ref[...]

    before = (iota((units, units), 0) < iota((units, units), 1)).astype(BF16)
    pair = lax.shift_right_logical(node, 1)
    group = iota((PAIRS, units), 0)
    in_pair = ((group == pair) & (honest == 1)).astype(F32)
    held = jnp.minimum(jnp.sum(in_pair, axis=1, keepdims=True), float(room))
    index = jnp.sum(in_pair * dot(in_pair, before), axis=0, keepdims=True)
    placed = (honest == 1) & (index < room)
    filler = jnp.broadcast_to(jnp.where(placed, 0.0, 1.0), (8, units))
    filler_rank = dot(filler, before)[0:1]
    free = jnp.broadcast_to(room - held, (PAIRS, units))
    lower = (iota((PAIRS, PAIRS), 1) < iota((PAIRS, PAIRS), 0)).astype(BF16)
    first = dot(lower, free)
    in_gap = (filler_rank >= first) & (filler_rank < first + free)
    gap_lane = jnp.sum(
        jnp.where(in_gap, group.astype(F32) * room + held - first + filler_rank, 0.0), axis=0, keepdims=True
    )
    lane = jnp.where(placed, pair * room + index.astype(jnp.int32), gap_lane.astype(jnp.int32))
    lane = lane ^ (room * (me & 3))
    place = jnp.where(iota((units, units), 0) == lane, 1.0, 0.0).astype(BF16)

    keys = jnp.concatenate(
        [node.astype(F32), arm.astype(F32), honest.astype(F32), jnp.zeros((5, units), F32)], axis=0
    )
    wide = jnp.concatenate([outcome_ref[...].astype(F32), codes_ref[...].astype(F32), keys], axis=0)
    sorted_wide = dot(wide, place, NT)
    sorted_keys = sorted_wide[weeks + covars :]

    flat = jnp.concatenate([chosen_ref[n : n + 1, :] for n in range(NODES)], axis=1)
    hot = jnp.where(iota((covars, NODES * slots), 0) == flat, 1.0, 0.0)
    per_node = dot(hot, sorted_wide[weeks : weeks + covars], (((0,), (0,)), ((), ())))
    picked = jnp.zeros((slots, units), F32)
    for n in range(NODES):
        picked = picked + jnp.where(sorted_keys[0:1] == float(n), per_node[n * slots : (n + 1) * slots], 0.0)
    for j in range(owners):
        scratch[j, 0:per_owner] = picked[j * per_owner : (j + 1) * per_owner]

    half = owners // 2
    assert rows == weeks + 8
    for start, out in ((0, own_ref), (half, away_ref)):
        mine = [scratch[me ^ (start + j)][0:per_owner] for j in range(half)]
        out[0:rows] = jnp.concatenate(
            [sorted_wide[0:weeks], sorted_keys[0:4], mine[0], sorted_keys[4 + per_owner :]][: 3 + (per_owner < 4)], axis=0
        ).astype(BF16)
        out[rows:] = jnp.concatenate(mine, axis=0).astype(BF16)


def gain_kernel(layout, weeks, per_owner, *refs):
    n_in = len(layout)
    blocks = refs[:n_in]
    gain_ref, effect_ref, outs, keys, sums = refs[n_in:]
    depth = outs.shape[2]
    me = lax.axis_index("row")
    where_of = {k: (ref, at) for ref, ids in zip(blocks, layout) for at, k in enumerate(ids)}
    n_blocks = len(where_of)
    rows = block_rows(weeks, per_owner)
    quarter = lax.shift_right_logical(iota((8, LANES), 1), 5) ^ (me & 3)
    masks = [quarter == t for t in range(4)]
    bins_up = (iota((BINS, depth), 0) + 1).astype(F32).astype(BF16)
    one, zero = jnp.ones((), BF16), jnp.zeros((), BF16)

    def loaded(k, half):
        ref, at = where_of[k]
        return ref[at, 0:rows, half * LANES : (half + 1) * LANES].astype(F32)

    def week_rows(g, out, key):
        node, arm, honest = key[0:1], key[1:2], key[2:3]
        mine, counts = [], []
        for m in range(2):
            of_node = (node == (2 * g + m).astype(F32)) & (honest == 1.0)
            for a in (1.0, 0.0):
                here = jnp.where(of_node & (arm == a), 1.0, 0.0)
                mine.append(out * here)
                counts.append(jnp.broadcast_to(here, (8, here.shape[1])))
        return jnp.concatenate(mine + counts, axis=0).astype(BF16)

    def step_rows(key, s):
        pick = jnp.broadcast_to(key[4 + s : 5 + s], (16, key.shape[1])).astype(BF16)
        pick = jnp.concatenate([pick] * (BINS // 16), axis=0)
        return jnp.maximum(jnp.minimum(bins_up - pick, one), zero)

    def pair_gains(left, total):
        gains = []
        for m in range(2):
            base, count = 2 * m * weeks, 4 * weeks + 16 * m
            treated, control = left[base : base + weeks], left[base + weeks : base + 2 * weeks]
            all_treated, all_control = total[base : base + weeks], total[base + weeks : base + 2 * weeks]
            lt, lc = left[count : count + 8], left[count + 8 : count + 16]
            rt, rc = total[count : count + 8] - lt, total[count + 8 : count + 16] - lc
            it, ic = 1.0 / (rt + 1.0), 1.0 / (rc + 1.0)
            at, ac = 1.0 / (lt + 1.0) + it, 1.0 / (lc + 1.0) + ic
            spread = None
            for w in range(0, weeks, 8):
                rng = slice(w, w + 8)
                gap = (treated[rng] * at - all_treated[rng] * it) - (control[rng] * ac - all_control[rng] * ic)
                spread = gap * gap if spread is None else spread + gap * gap
            cl, cr = lt + lc, rt + rc
            balance = cl * cr / ((cl + cr + 1.0) * (cl + cr + 1.0))
            gains.append(jnp.sum(balance * spread, axis=0, keepdims=True))
        return gains

    def last_bin(left):
        return jnp.broadcast_to(left[:, BINS - 1 : BINS], left.shape)

    strays = jnp.zeros((1, depth), F32)
    est = jnp.zeros((2 * NODES, weeks), F32)
    est_units = jnp.zeros((2 * NODES, depth), F32)
    for half in range(2):
        held = [loaded(k, half) for k in range(n_blocks)]
        for g in range(half * 4, half * 4 + 4):
            parts = []
            for first in range(0, n_blocks, 4):
                part = held[first]
                for k in range(first + 1, first + 4):
                    mask = jnp.concatenate([masks[(g ^ k) & 3]] * (part.shape[0] // 8), axis=0)
                    part = jnp.where(mask, held[k], part)
                parts.append(part)
            block = jnp.concatenate(parts, axis=1)
            out, key = block[0:weeks], block[weeks : weeks + 8]
            outs[g] = out
            keys[g] = key
            node, arm, honest = key[0:1], key[1:2], key[2:3]
            strays = strays + jnp.where((honest == 1.0) & ((node < 2.0 * g) | (node > 2.0 * g + 1.0)), 1.0, 0.0)
            kept = jnp.where(honest == 0.0, node, -1.0)
            kept_hot = kept == iota((NODES, depth), 0).astype(F32)
            hot = jnp.concatenate(
                [jnp.where(kept_hot & (arm == a), 1.0, 0.0) for a in (1.0, 0.0)], axis=0
            )
            est = est + dot(hot, out, NT)
            est_units = est_units + hot
            mine = week_rows(jnp.int32(g), out, key)
            total = None
            for s in range(per_owner):
                left = dot(mine, step_rows(key, s), NT)
                total = last_bin(left) if total is None else total
                for m, gain in enumerate(pair_gains(left, total)):
                    gain_ref[s, 2 * g + m : 2 * g + m + 1] = gain

    units = jnp.sum(est_units, axis=1, keepdims=True)
    effect_ref[...] = est / (units + 1.0)

    @pl.when(jnp.sum(strays) > 0.0)
    def _():
        def over_pairs(g, carry):
            for s in range(per_owner):
                sums[...] = jnp.zeros_like(sums)

                def over_lanes(other, carry):
                    sums[...] += dot(week_rows(g, outs[other], keys[other]), step_rows(keys[other], s), NT)
                    return carry

                lax.fori_loop(0, PAIRS, over_lanes, 0)
                left = sums[...]
                for m, gain in enumerate(pair_gains(left, last_bin(left))):
                    gain_ref[s, pl.ds(2 * g + m, 1)] = gain
            return carry

        lax.fori_loop(0, PAIRS, over_pairs, 0)


def shards(codes, node, chosen, arm, honest, outcome):
    units, weeks = outcome.shape
    slots = chosen.shape[1]
    owners, periods = lax.axis_size("row"), lax.axis_size("period")
    per_owner = slots // owners
    rows = block_rows(weeks, per_owner)
    vmem = pl.BlockSpec(memory_space=pltpu.VMEM)

    def swap(x, axis, bit):
        return lax.ppermute(x, axis, [(i, i ^ bit) for i in range(lax.axis_size(axis))])

    packed = jax.ShapeDtypeStruct((rows + slots // 2, units), BF16)
    inputs = (codes.T, node.reshape(1, units), arm.reshape(1, units), honest.reshape(1, units), chosen, outcome.T)
    own, away = pl.pallas_call(
        functools.partial(pack_kernel, owners),
        out_shape=(packed, packed),
        in_specs=[vmem] * 6,
        out_specs=(vmem, vmem),
        compiler_params=pltpu.CompilerParams(vmem_limit_bytes=8 * 1024 * 1024),
        scratch_shapes=[pltpu.VMEM((owners, -(-per_owner // 8) * 8, units), F32)],
    )(*(pltpu.with_memory_space_constraint(x, pltpu.HBM) for x in inputs))

    def part(x, first, last):
        bins = x[:, rows + first * per_owner : rows + last * per_owner]
        block = [x[:, : weeks + 4], bins[:, :per_owner], x[:, weeks + 4 + per_owner : rows]]
        return jnp.concatenate(block + ([bins] if last > first + 1 else []), axis=1)

    groups, bit = owners // 2, owners // 2
    held = [(own[None], [0]), (swap(away, "row", bit)[None], [bit])]
    while groups > 4:
        groups, bit = groups // 2, bit // 2
        ids = [k for _, some in held for k in some]
        send = jnp.concatenate([part(x, groups, 2 * groups) for x, _ in held], axis=0)
        keep = jnp.concatenate([x[:, : rows + groups * per_owner] for x, _ in held], axis=0)
        held = [(keep, ids), (swap(send, "row", bit), [k ^ bit for k in ids])]
    ids = [k for _, some in held for k in some]
    layout = [some for _, some in held]
    blocks = [x for x, _ in held]
    for k in (3, 2, 1):
        send = jnp.concatenate([part(x, k, k + 1) for x, _ in held], axis=0)
        blocks.append(swap(send, "row", k))
        layout.append([i ^ k for i in ids])

    depth = owners * units // PAIRS
    gain, effect = pl.pallas_call(
        functools.partial(gain_kernel, layout, weeks, per_owner),
        out_shape=(jax.ShapeDtypeStruct((per_owner, NODES, BINS), F32), jax.ShapeDtypeStruct((2 * NODES, weeks), F32)),
        in_specs=[vmem] * len(blocks),
        out_specs=(vmem, vmem),
        scratch_shapes=[
            pltpu.VMEM((PAIRS, weeks, depth), F32),
            pltpu.VMEM((PAIRS, 8, depth), F32),
            pltpu.VMEM((4 * weeks + 32, BINS), F32),
        ],
        compiler_params=pltpu.CompilerParams(vmem_limit_bytes=16 * 1024 * 1024),
    )(*blocks)

    gain = gain + swap(gain, "period", 1)
    bit = 2
    while bit < periods:
        gain = gain + swap(gain, "period", bit | 1)
        bit *= 2
    share = BINS // periods
    gains = lax.dynamic_slice_in_dim(gain, lax.axis_index("period") * share, share, 2)
    best = jnp.max(gain, axis=(0, 2))
    bit = 1
    while bit < owners:
        best = jnp.maximum(best, swap(best, ("row", "period"), bit * periods | 1))
        bit *= 2
    return gains, best, effect[:NODES] - effect[NODES:]


def solution(mesh):
    in_specs = (P("row", None), P("row"), P(), P("row"), P("row"), P("row", "period"))
    out_specs = (P("row", None, "period"), P(), P(None, "period"))
    return jax.shard_map(shards, mesh=mesh, in_specs=in_specs, out_specs=out_specs, check_vma=False)
```

```python
import functools

import jax
import jax.numpy as jnp
from jax import lax
from jax.experimental import pallas as pl
from jax.experimental.pallas import tpu as pltpu
from jax.sharding import PartitionSpec as P

NODES = 16
BINS = 256
LANES = 128
PAIRS = NODES // 2
BF16 = jnp.bfloat16
F32 = jnp.float32
NT = (((1,), (1,)), ((), ()))


def iota(shape, axis):
    return lax.broadcasted_iota(jnp.int32, shape, axis)


def dot(a, b, dims=(((1,), (0,)), ((), ()))):
    return lax.dot_general(a.astype(BF16), b.astype(BF16), dims, preferred_element_type=F32)


def place_kernel(owners, codes_ref, node_ref, arm_ref, honest_ref, chosen_ref, outcome_ref, place_ref, mine_ref, scratch):
    covars, units = codes_ref.shape
    slots, weeks = chosen_ref.shape[1], outcome_ref.shape[0]
    per_owner = slots // owners
    room = units // PAIRS
    me = lax.axis_index("row")
    node, arm, honest = node_ref[...], arm_ref[...], honest_ref[...]

    before = (iota((units, units), 0) < iota((units, units), 1)).astype(BF16)
    pair = lax.shift_right_logical(node, 1)
    group = iota((PAIRS, units), 0)
    in_pair = ((group == pair) & (honest == 1)).astype(F32)
    earlier = dot(in_pair, before)
    index = jnp.sum(in_pair * earlier, axis=0, keepdims=True)
    placed = (honest == 1) & (index < room)
    placed_earlier = jnp.sum(jnp.minimum(earlier, float(room)), axis=0, keepdims=True)
    filler_rank = iota((1, units), 1).astype(F32) - placed_earlier
    held = jnp.minimum(jnp.sum(in_pair, axis=1, keepdims=True), float(room))
    free = jnp.broadcast_to(room - held, (PAIRS, units))
    first = free
    for step in (1, 2, 4):
        first = first + jnp.concatenate([jnp.zeros((step, units), F32), first[: PAIRS - step]], axis=0)
    first = first - free
    in_gap = (filler_rank >= first) & (filler_rank < first + free)
    gap_lane = jnp.sum(
        jnp.where(in_gap, group.astype(F32) * room + held - first + filler_rank, 0.0), axis=0, keepdims=True
    )
    lane = jnp.where(placed, pair * room + index.astype(jnp.int32), gap_lane.astype(jnp.int32))
    lane = lane ^ (room * (me & 3))
    place = jnp.where(iota((units, units), 0) == lane, 1.0, 0.0).astype(BF16)
    place_ref[...] = place

    flat = jnp.concatenate([chosen_ref[n : n + 1, :] for n in range(NODES)], axis=1)
    hot = jnp.where(iota((covars, NODES * slots), 0) == flat, 1.0, 0.0)
    per_node = dot(hot, codes_ref[...].astype(F32), (((0,), (0,)), ((), ())))
    picked = jnp.zeros((slots, units), F32)
    for n in range(NODES):
        picked = picked + jnp.where(node == n, per_node[n * slots : (n + 1) * slots], 0.0)
    for j in range(owners):
        scratch[j, 0:per_owner] = picked[j * per_owner : (j + 1) * per_owner]
    ordered = [scratch[me ^ j ^ k][0:per_owner] for j in range(owners // 2) for k in (0, owners // 2)]

    keys = [node.astype(F32), arm.astype(F32), honest.astype(F32), jnp.zeros((1, units), F32)]
    wide = jnp.concatenate([outcome_ref[...].astype(F32), *keys, *ordered, jnp.zeros((4, units), F32)], axis=0)
    mine_ref[...] = dot(wide, place, NT)


def join_kernel(per_owner, place_ref, mine_ref, other_ref, own_ref, away_ref):
    weeks = other_ref.shape[0]
    mine = mine_ref[...]
    tail = mine[weeks:]
    outcome, other = mine[0:weeks], dot(other_ref[...], place_ref[...], NT)
    first = (lax.axis_index("period") & 1) == 0
    both = [jnp.where(first, outcome, other), jnp.where(first, other, outcome)]
    own_ref[...] = jnp.concatenate([*both, tail], axis=0).astype(BF16)
    turned = [
        tail[at : at + per_owner]
        for pair in range(4, tail.shape[0] - 4, 2 * per_owner)
        for at in (pair + per_owner, pair)
    ]
    away_ref[...] = jnp.concatenate([*both, tail[0:4], *turned, tail[-4:]], axis=0).astype(BF16)


def gain_kernel(layout, per_owner, periods, *refs):
    n_in = len(layout)
    blocks = refs[:n_in]
    gain_ref, effect_ref, outs, keys, sums = refs[n_in:]
    weeks, depth, key_rows = outs.shape[1], outs.shape[2], keys.shape[1]
    me, period = lax.axis_index("row"), lax.axis_index("period")
    where_of = {k: (ref, at) for ref, ids in zip(blocks, layout) for at, k in enumerate(ids)}
    n_blocks = len(where_of)
    quarter = lax.shift_right_logical(iota((8, LANES), 1), 5) ^ (me & 3)
    masks = [quarter == t for t in range(4)]
    one, zero = jnp.ones((), BF16), jnp.zeros((), BF16)

    share = BINS // periods
    row = iota((BINS // 2, depth), 0)
    index, within = row // share, row % share
    odd = period ^ index
    for shift in (2, 1):
        odd = odd ^ lax.shift_right_logical(odd, shift)
    bins_up = ((2 * index + (odd & 1)) * share + within + 1).astype(F32).astype(BF16)

    def loaded(k, half):
        ref, at = where_of[k]
        return ref[at, 0 : weeks + key_rows, half * LANES : (half + 1) * LANES].astype(F32)

    def week_rows(g, out, key):
        node, arm, honest = key[0:1], key[1:2], key[2:3]
        mine, counts = [], []
        for m in range(2):
            of_node = (node == (2 * g + m).astype(F32)) & (honest == 1.0)
            for a in (1.0, 0.0):
                here = jnp.where(of_node & (arm == a), 1.0, 0.0)
                mine.append(out * here)
                counts.append(jnp.broadcast_to(here, (8, here.shape[1])))
        return jnp.concatenate(mine + counts, axis=0)

    def step_rows(key, tile):
        steps = []
        for s in (2 * tile, 2 * tile + 1):
            pick = jnp.broadcast_to(key[4 + s : 5 + s], (16, key.shape[1])).astype(BF16)
            pick = jnp.concatenate([pick] * (BINS // 32), axis=0)
            steps.append(jnp.maximum(jnp.minimum(bins_up - pick, one), zero))
        return jnp.concatenate(steps, axis=0)

    def pair_gains(left, total):
        gains = []
        for m in range(2):
            base, count = 2 * m * weeks, 4 * weeks + 16 * m
            treated, control = left[base : base + weeks], left[base + weeks : base + 2 * weeks]
            all_treated, all_control = total[base : base + weeks], total[base + weeks : base + 2 * weeks]
            lt, lc = left[count : count + 8], left[count + 8 : count + 16]
            rt, rc = total[count : count + 8] - lt, total[count + 8 : count + 16] - lc
            it, ic = 1.0 / (rt + 1.0), 1.0 / (rc + 1.0)
            at, ac = 1.0 / (lt + 1.0) + it, 1.0 / (lc + 1.0) + ic
            spread = None
            for w in range(0, weeks, 8):
                rng = slice(w, w + 8)
                gap = (treated[rng] * at - all_treated[rng] * it) - (control[rng] * ac - all_control[rng] * ic)
                spread = gap * gap if spread is None else spread + gap * gap
            cl, cr = lt + lc, rt + rc
            balance = cl * cr / ((cl + cr + 1.0) * (cl + cr + 1.0))
            gains.append(jnp.sum(balance * spread, axis=0, keepdims=True))
        return gains

    def totals(mine):
        return jnp.broadcast_to(jnp.sum(mine, axis=1, keepdims=True), (mine.shape[0], BINS))

    def store(tile, rows, gain):
        gain_ref[2 * tile, rows] = gain[:, : BINS // 2]
        gain_ref[2 * tile + 1, rows] = gain[:, BINS // 2 :]

    strays = jnp.zeros((1, depth), F32)
    est = jnp.zeros((2 * NODES, weeks // 2), F32)
    est_units = jnp.zeros((2 * NODES, depth), F32)
    for half in range(2):
        held = [loaded(k, half) for k in range(n_blocks)]
        for g in range(half * 4, half * 4 + 4):
            parts = []
            for first in range(0, n_blocks, 4):
                part = held[first]
                for k in range(first + 1, first + 4):
                    mask = jnp.concatenate([masks[(g ^ k) & 3]] * (part.shape[0] // 8), axis=0)
                    part = jnp.where(mask, held[k], part)
                parts.append(part)
            block = jnp.concatenate(parts, axis=1)
            out, key = block[0:weeks], block[weeks:]
            outs[g] = out
            keys[g] = key
            node, arm, honest = key[0:1], key[1:2], key[2:3]
            strays = strays + jnp.where((honest == 1.0) & ((node < 2.0 * g) | (node > 2.0 * g + 1.0)), 1.0, 0.0)
            kept = jnp.where(honest == 0.0, node, -1.0)
            kept_hot = kept == iota((NODES, depth), 0).astype(F32)
            hot = jnp.concatenate(
                [jnp.where(kept_hot & (arm == a), 1.0, 0.0) for a in (1.0, 0.0)], axis=0
            )
            est = est + dot(hot, jnp.where((period & 1) == 0, out[: weeks // 2], out[weeks // 2 :]), NT)
            est_units = est_units + hot
            mine = week_rows(jnp.int32(g), out, key)
            total = totals(mine)
            for tile in range(per_owner):
                left = dot(mine, step_rows(key, tile), NT)
                for m, gain in enumerate(pair_gains(left, total)):
                    store(tile, slice(2 * g + m, 2 * g + m + 1), gain)

    units = jnp.sum(est_units, axis=1, keepdims=True)
    effect_ref[...] = est / (units + 1.0)

    @pl.when(jnp.sum(strays) > 0.0)
    def _():
        def over_pairs(g, carry):
            for tile in range(per_owner):
                sums[...] = jnp.zeros_like(sums)

                def over_lanes(other, total):
                    mine = week_rows(g, outs[other], keys[other])
                    sums[...] += dot(mine, step_rows(keys[other], tile), NT)
                    return total + totals(mine)

                total = lax.fori_loop(0, PAIRS, over_lanes, jnp.zeros(sums.shape, F32))
                for m, gain in enumerate(pair_gains(sums[...], total)):
                    store(tile, pl.ds(2 * g + m, 1), gain)
            return carry

        lax.fori_loop(0, PAIRS, over_pairs, 0)


def shards(codes, node, chosen, arm, honest, outcome):
    units, weeks = outcome.shape
    slots = chosen.shape[1]
    owners, periods = lax.axis_size("row"), lax.axis_size("period")
    per_owner = slots // owners
    vmem = pl.BlockSpec(memory_space=pltpu.VMEM)

    def swap(x, axis, bit):
        return lax.ppermute(x, axis, [(i, i ^ bit) for i in range(lax.axis_size(axis))])

    def cross(x, bit):
        return swap(x, ("row", "period"), bit * periods | 1)

    inputs = (codes.T, node.reshape(1, units), arm.reshape(1, units), honest.reshape(1, units), chosen, outcome.T)
    other = swap(outcome.T, "period", 1)
    place, mine = pl.pallas_call(
        functools.partial(place_kernel, owners),
        out_shape=(
            jax.ShapeDtypeStruct((units, units), BF16),
            jax.ShapeDtypeStruct((weeks + 8 + slots, units), F32),
        ),
        in_specs=[vmem] * 6,
        out_specs=(vmem, vmem),
        compiler_params=pltpu.CompilerParams(vmem_limit_bytes=8 * 1024 * 1024),
        scratch_shapes=[pltpu.VMEM((owners, -(-per_owner // 8) * 8, units), F32)],
    )(*(pltpu.with_memory_space_constraint(x, pltpu.HBM) for x in inputs))
    packed = jax.ShapeDtypeStruct((2 * weeks + 8 + slots, units), BF16)
    own, away = pl.pallas_call(
        functools.partial(join_kernel, per_owner),
        out_shape=(packed, packed),
        in_specs=[vmem] * 3,
        out_specs=(vmem, vmem),
        compiler_params=pltpu.CompilerParams(vmem_limit_bytes=4 * 1024 * 1024),
    )(place, mine, other)

    bins_at, width = 2 * weeks + 4, 2 * per_owner
    key_rows = -(-(4 + width) // 8) * 8

    def part(x, first, last, more):
        return jnp.concatenate([x[:, :bins_at], x[:, bins_at + first * width : bins_at + last * width + more]], axis=1)

    half = owners // 2
    held = [(own[None], [0]), (cross(away, half)[None], [half])]
    groups = half
    while groups > 4:
        groups //= 2
        ids = [k for _, some in held for k in some]
        whole = jnp.concatenate([x for x, _ in held], axis=0)
        came = cross(part(whole, groups, 2 * groups, 4), groups)
        held = [(part(whole, 0, groups, 4), ids), (came, [k ^ groups for k in ids])]
    ids = [k for _, some in held for k in some]
    layout = [some for _, some in held]
    blocks = [x for x, _ in held]
    for k in (3, 2, 1):
        send = jnp.concatenate([part(x, k, k + 1, key_rows - 4 - width) for x, _ in held], axis=0)
        blocks.append(cross(send, k))
        layout.append([i ^ k for i in ids])

    depth = owners * units // PAIRS
    gain, effect = pl.pallas_call(
        functools.partial(gain_kernel, layout, per_owner, periods),
        out_shape=(
            jax.ShapeDtypeStruct((2 * per_owner, NODES, BINS // 2), F32),
            jax.ShapeDtypeStruct((2 * NODES, weeks), F32),
        ),
        in_specs=[vmem] * len(blocks),
        out_specs=(vmem, vmem),
        scratch_shapes=[
            pltpu.VMEM((PAIRS, 2 * weeks, depth), F32),
            pltpu.VMEM((PAIRS, key_rows, depth), F32),
            pltpu.VMEM((8 * weeks + 32, BINS), F32),
        ],
        compiler_params=pltpu.CompilerParams(vmem_limit_bytes=16 * 1024 * 1024),
    )(*blocks)

    bit = 2
    while bit < periods:
        gain = gain + swap(gain, "period", bit | 1)
        bit *= 2
    share = BINS // periods
    gains = lax.dynamic_slice_in_dim(gain[:per_owner], (lax.axis_index("period") >> 1) * share, share, 2)
    best = jnp.max(gain, axis=(0, 2))
    best = jnp.maximum(best, swap(best, "period", 1))
    bit = 1
    while bit < half:
        best = jnp.maximum(best, cross(best, bit))
        bit *= 2
    return gains, best, effect[:NODES] - effect[NODES:]


def solution(mesh):
    in_specs = (P("row", None), P("row"), P(), P("row"), P("row"), P("row", "period"))
    out_specs = (P("row", None, "period"), P(), P(None, "period"))
    return jax.shard_map(shards, mesh=mesh, in_specs=in_specs, out_specs=out_specs, check_vma=False)
```

```python
import functools

import jax
import jax.numpy as jnp
from jax import lax
from jax.experimental import pallas as pl
from jax.experimental.pallas import tpu as pltpu
from jax.sharding import PartitionSpec as P

NODES = 16
BINS = 256
LANES = 128
PAIRS = NODES // 2
BF16 = jnp.bfloat16
F32 = jnp.float32
NT = (((1,), (1,)), ((), ()))


def iota(shape, axis):
    return lax.broadcasted_iota(jnp.int32, shape, axis)


def dot(a, b, dims=(((1,), (0,)), ((), ()))):
    return lax.dot_general(a.astype(BF16), b.astype(BF16), dims, preferred_element_type=F32)


def place_kernel(owners, codes_ref, node_ref, arm_ref, honest_ref, chosen_ref, outcome_ref, place_ref, mine_ref, scratch):
    covars, units = codes_ref.shape
    slots, weeks = chosen_ref.shape[1], outcome_ref.shape[0]
    per_owner = slots // owners
    room = units // PAIRS
    me = lax.axis_index("row")
    node, arm, honest = node_ref[...], arm_ref[...], honest_ref[...]

    before = (iota((units, units), 0) < iota((units, units), 1)).astype(BF16)
    pair = lax.shift_right_logical(node, 1)
    group = iota((PAIRS, units), 0)
    in_pair = ((group == pair) & (honest == 1)).astype(F32)
    earlier = dot(in_pair, before)
    index = jnp.sum(in_pair * earlier, axis=0, keepdims=True)
    placed = (honest == 1) & (index < room)
    placed_earlier = jnp.sum(jnp.minimum(earlier, float(room)), axis=0, keepdims=True)
    filler_rank = iota((1, units), 1).astype(F32) - placed_earlier
    held = jnp.minimum(jnp.sum(in_pair, axis=1, keepdims=True), float(room))
    free = jnp.broadcast_to(room - held, (PAIRS, units))
    first = free
    for step in (1, 2, 4):
        first = first + jnp.concatenate([jnp.zeros((step, units), F32), first[: PAIRS - step]], axis=0)
    first = first - free
    in_gap = (filler_rank >= first) & (filler_rank < first + free)
    gap_lane = jnp.sum(
        jnp.where(in_gap, group.astype(F32) * room + held - first + filler_rank, 0.0), axis=0, keepdims=True
    )
    lane = jnp.where(placed, pair * room + index.astype(jnp.int32), gap_lane.astype(jnp.int32))
    lane = lane ^ (room * (me & 3))
    place = jnp.where(iota((units, units), 0) == lane, 1.0, 0.0).astype(BF16)
    place_ref[...] = place

    flat = jnp.concatenate([chosen_ref[n : n + 1, :] for n in range(NODES)], axis=1)
    hot = jnp.where(iota((covars, NODES * slots), 0) == flat, 1.0, 0.0)
    per_node = dot(hot, codes_ref[...].astype(F32), (((0,), (0,)), ((), ())))
    picked = jnp.zeros((slots, units), F32)
    for n in range(NODES):
        picked = picked + jnp.where(node == n, per_node[n * slots : (n + 1) * slots], 0.0)
    for j in range(owners):
        scratch[j, 0:per_owner] = picked[j * per_owner : (j + 1) * per_owner]
    ordered = [scratch[me ^ j ^ k][0:per_owner] for j in range(owners // 2) for k in (0, owners // 2)]

    keys = [node.astype(F32), arm.astype(F32), honest.astype(F32), jnp.zeros((1, units), F32)]
    wide = jnp.concatenate([outcome_ref[...].astype(F32), *keys, *ordered, jnp.zeros((4, units), F32)], axis=0)
    mine_ref[...] = dot(wide, place, NT)


def join_kernel(per_owner, place_ref, mine_ref, other_ref, own_ref, away_ref):
    weeks = other_ref.shape[0]
    mine = mine_ref[...]
    tail = mine[weeks:]
    outcome, other = mine[0:weeks], dot(other_ref[...], place_ref[...], NT)
    first = (lax.axis_index("period") & 1) == 0
    both = [jnp.where(first, outcome, other), jnp.where(first, other, outcome)]
    own_ref[...] = jnp.concatenate([*both, tail], axis=0).astype(BF16)
    turned = [
        tail[at : at + per_owner]
        for pair in range(4, tail.shape[0] - 4, 2 * per_owner)
        for at in (pair + per_owner, pair)
    ]
    away_ref[...] = jnp.concatenate([*both, tail[0:4], *turned, tail[-4:]], axis=0).astype(BF16)


def gain_kernel(layout, per_owner, periods, *refs):
    n_in = len(layout)
    blocks = refs[:n_in]
    gain_ref, effect_ref, outs, keys, sums = refs[n_in:]
    weeks, depth, key_rows = outs.shape[1], outs.shape[2], keys.shape[1]
    me, period = lax.axis_index("row"), lax.axis_index("period")
    where_of = {k: (ref, at) for ref, ids in zip(blocks, layout) for at, k in enumerate(ids)}
    n_blocks = len(where_of)
    quarter = lax.shift_right_logical(iota((8, LANES), 1), 5) ^ (me & 3)
    masks = [quarter == t for t in range(4)]
    one, zero = jnp.ones((), BF16), jnp.zeros((), BF16)

    share = BINS // periods
    row = iota((BINS // 2, depth), 0)
    index, within = row // share, row % share
    odd = period ^ index
    for shift in (2, 1):
        odd = odd ^ lax.shift_right_logical(odd, shift)
    bins_up = ((2 * index + (odd & 1)) * share + within + 1).astype(F32).astype(BF16)

    def loaded(k, half):
        ref, at = where_of[k]
        return ref[at, 0 : weeks + key_rows, half * LANES : (half + 1) * LANES].astype(F32)

    def week_rows(g, out, key):
        node, arm, honest = key[0:1], key[1:2], key[2:3]
        mine, counts = [], []
        for m in range(2):
            of_node = (node == (2 * g + m).astype(F32)) & (honest == 1.0)
            arms = [jnp.where(of_node & (arm == a), 1.0, 0.0) for a in (1.0, 0.0)]
            counts += [jnp.broadcast_to(here, (8, here.shape[1])) for here in arms]
            mine += [out[w : w + 8] * here for w in range(0, weeks, 8) for here in arms]
        return jnp.concatenate(counts + mine, axis=0)

    def step_rows(key, tile):
        steps = []
        for s in (2 * tile, 2 * tile + 1):
            pick = jnp.broadcast_to(key[4 + s : 5 + s], (16, key.shape[1])).astype(BF16)
            pick = jnp.concatenate([pick] * (BINS // 32), axis=0)
            steps.append(jnp.maximum(jnp.minimum(bins_up - pick, one), zero))
        return jnp.concatenate(steps, axis=0)

    def pair_gains(left, total):
        gains = []
        for m in range(2):
            base, count = 32 + 2 * m * weeks, 16 * m
            lt, lc = left[count : count + 8], left[count + 8 : count + 16]
            rt, rc = total[count : count + 8] - lt, total[count + 8 : count + 16] - lc
            it, ic = 1.0 / (rt + 1.0), 1.0 / (rc + 1.0)
            at, ac = 1.0 / (lt + 1.0) + it, 1.0 / (lc + 1.0) + ic
            spread = None
            for w in range(base, base + 2 * weeks, 16):
                treated, control = slice(w, w + 8), slice(w + 8, w + 16)
                gap = (left[treated] * at - total[treated] * it) - (left[control] * ac - total[control] * ic)
                spread = gap * gap if spread is None else spread + gap * gap
            cl, cr = lt + lc, rt + rc
            balance = cl * cr / ((cl + cr + 1.0) * (cl + cr + 1.0))
            gains.append(jnp.sum(balance * spread, axis=0, keepdims=True))
        return gains

    def totals(mine):
        return jnp.broadcast_to(jnp.sum(mine, axis=1, keepdims=True), (mine.shape[0], BINS // 2))

    def store(tile, nodes, left, total):
        for h in range(2):
            for m, gain in enumerate(pair_gains(left[:, h * BINS // 2 : (h + 1) * BINS // 2], total)):
                gain_ref[2 * tile + h, nodes[m]] = gain

    strays = jnp.zeros((1, depth), F32)
    est = jnp.zeros((2 * NODES, weeks // 2), F32)
    est_units = jnp.zeros((2 * NODES, depth), F32)
    for half in range(2):
        held = [loaded(k, half) for k in range(n_blocks)]
        for g in range(half * 4, half * 4 + 4):
            parts = []
            for first in range(0, n_blocks, 4):
                part = held[first]
                for k in range(first + 1, first + 4):
                    mask = jnp.concatenate([masks[(g ^ k) & 3]] * (part.shape[0] // 8), axis=0)
                    part = jnp.where(mask, held[k], part)
                parts.append(part)
            block = jnp.concatenate(parts, axis=1)
            out, key = block[0:weeks], block[weeks:]
            outs[g] = out
            keys[g] = key
            node, arm, honest = key[0:1], key[1:2], key[2:3]
            strays = strays + jnp.where((honest == 1.0) & ((node < 2.0 * g) | (node > 2.0 * g + 1.0)), 1.0, 0.0)
            kept = jnp.where(honest == 0.0, node, -1.0)
            kept_hot = kept == iota((NODES, depth), 0).astype(F32)
            hot = jnp.concatenate(
                [jnp.where(kept_hot & (arm == a), 1.0, 0.0) for a in (1.0, 0.0)], axis=0
            )
            est = est + dot(hot, jnp.where((period & 1) == 0, out[: weeks // 2], out[weeks // 2 :]), NT)
            est_units = est_units + hot
            mine = week_rows(jnp.int32(g), out, key)
            total = totals(mine)
            lefts = [dot(mine, step_rows(key, tile), NT) for tile in range(per_owner)]
            for tile, left in enumerate(lefts):
                store(tile, [slice(2 * g + m, 2 * g + m + 1) for m in range(2)], left, total)

    units = jnp.sum(est_units, axis=1, keepdims=True)
    effect_ref[...] = est / (units + 1.0)

    @pl.when(jnp.sum(strays) > 0.0)
    def _():
        def over_pairs(g, carry):
            for tile in range(per_owner):
                sums[...] = jnp.zeros_like(sums)

                def over_lanes(other, total):
                    mine = week_rows(g, outs[other], keys[other])
                    sums[...] += dot(mine, step_rows(keys[other], tile), NT)
                    return total + totals(mine)

                total = lax.fori_loop(0, PAIRS, over_lanes, jnp.zeros((sums.shape[0], BINS // 2), F32))
                store(tile, [pl.ds(2 * g + m, 1) for m in range(2)], sums[...], total)
            return carry

        lax.fori_loop(0, PAIRS, over_pairs, 0)


def shards(codes, node, chosen, arm, honest, outcome):
    units, weeks = outcome.shape
    slots = chosen.shape[1]
    owners, periods = lax.axis_size("row"), lax.axis_size("period")
    per_owner = slots // owners
    vmem = pl.BlockSpec(memory_space=pltpu.VMEM)

    def swap(x, axis, bit):
        return lax.ppermute(x, axis, [(i, i ^ bit) for i in range(lax.axis_size(axis))])

    def cross(x, bit):
        return swap(x, ("row", "period"), bit * periods | 1)

    inputs = (codes.T, node.reshape(1, units), arm.reshape(1, units), honest.reshape(1, units), chosen, outcome.T)
    other = swap(outcome.T, "period", 1)
    place, mine = pl.pallas_call(
        functools.partial(place_kernel, owners),
        out_shape=(
            jax.ShapeDtypeStruct((units, units), BF16),
            jax.ShapeDtypeStruct((weeks + 8 + slots, units), F32),
        ),
        in_specs=[vmem] * 6,
        out_specs=(vmem, vmem),
        compiler_params=pltpu.CompilerParams(vmem_limit_bytes=8 * 1024 * 1024),
        scratch_shapes=[pltpu.VMEM((owners, -(-per_owner // 8) * 8, units), F32)],
    )(*(pltpu.with_memory_space_constraint(x, pltpu.HBM) for x in inputs))
    packed = jax.ShapeDtypeStruct((2 * weeks + 8 + slots, units), BF16)
    own, away = pl.pallas_call(
        functools.partial(join_kernel, per_owner),
        out_shape=(packed, packed),
        in_specs=[vmem] * 3,
        out_specs=(vmem, vmem),
        compiler_params=pltpu.CompilerParams(vmem_limit_bytes=4 * 1024 * 1024),
    )(place, mine, other)

    bins_at, width = 2 * weeks + 4, 2 * per_owner
    key_rows = -(-(4 + width) // 8) * 8

    def part(x, first, last, more):
        return jnp.concatenate([x[:, :bins_at], x[:, bins_at + first * width : bins_at + last * width + more]], axis=1)

    half = owners // 2
    held = [(own[None], [0]), (cross(away, half)[None], [half])]
    groups = half
    while groups > 4:
        groups //= 2
        ids = [k for _, some in held for k in some]
        whole = jnp.concatenate([x for x, _ in held], axis=0)
        came = cross(part(whole, groups, 2 * groups, 4), groups)
        held = [(part(whole, 0, groups, 4), ids), (came, [k ^ groups for k in ids])]
    ids = [k for _, some in held for k in some]
    layout = [some for _, some in held]
    blocks = [x for x, _ in held]
    for k in (3, 2, 1):
        send = jnp.concatenate([part(x, k, k + 1, key_rows - 4 - width) for x, _ in held], axis=0)
        blocks.append(cross(send, k))
        layout.append([i ^ k for i in ids])

    depth = owners * units // PAIRS
    gain, effect = pl.pallas_call(
        functools.partial(gain_kernel, layout, per_owner, periods),
        out_shape=(
            jax.ShapeDtypeStruct((2 * per_owner, NODES, BINS // 2), F32),
            jax.ShapeDtypeStruct((2 * NODES, weeks), F32),
        ),
        in_specs=[vmem] * len(blocks),
        out_specs=(vmem, vmem),
        scratch_shapes=[
            pltpu.VMEM((PAIRS, 2 * weeks, depth), F32),
            pltpu.VMEM((PAIRS, key_rows, depth), F32),
            pltpu.VMEM((8 * weeks + 32, BINS), F32),
        ],
        compiler_params=pltpu.CompilerParams(vmem_limit_bytes=16 * 1024 * 1024),
    )(*blocks)

    bit = 2
    while bit < periods:
        gain = gain + swap(gain, "period", bit | 1)
        bit *= 2
    share = BINS // periods
    gains = lax.dynamic_slice_in_dim(gain[:per_owner], (lax.axis_index("period") >> 1) * share, share, 2)
    best = jnp.max(gain, axis=(0, 2))
    best = jnp.maximum(best, swap(best, "period", 1))
    bit = 1
    while bit < half:
        best = jnp.maximum(best, cross(best, bit))
        bit *= 2
    return gains, best, effect[:NODES] - effect[NODES:]


def solution(mesh):
    in_specs = (P("row", None), P("row"), P(), P("row"), P("row"), P("row", "period"))
    out_specs = (P("row", None, "period"), P(), P(None, "period"))
    return jax.shard_map(shards, mesh=mesh, in_specs=in_specs, out_specs=out_specs, check_vma=False)
```

```python
import functools

import jax
import jax.numpy as jnp
from jax import lax
from jax.experimental import pallas as pl
from jax.experimental.pallas import tpu as pltpu
from jax.sharding import PartitionSpec as P

NODES = 16
BINS = 256
LANES = 128
PAIRS = NODES // 2
BF16 = jnp.bfloat16
F32 = jnp.float32
NT = (((1,), (1,)), ((), ()))


def iota(shape, axis):
    return lax.broadcasted_iota(jnp.int32, shape, axis)


def dot(a, b, dims=(((1,), (0,)), ((), ()))):
    return lax.dot_general(a.astype(BF16), b.astype(BF16), dims, preferred_element_type=F32)


def place_kernel(owners, codes_ref, node_ref, arm_ref, honest_ref, chosen_ref, outcome_ref, place_ref, mine_ref, scratch):
    covars, units = codes_ref.shape
    slots, weeks = chosen_ref.shape[1], outcome_ref.shape[0]
    per_owner = slots // owners
    room = units // PAIRS
    me = lax.axis_index("row")
    node, arm, honest = node_ref[...], arm_ref[...], honest_ref[...]

    before = (iota((units, units), 0) < iota((units, units), 1)).astype(BF16)
    pair = lax.shift_right_logical(node, 1)
    group = iota((PAIRS, units), 0)
    in_pair = ((group == pair) & (honest == 1)).astype(F32)
    earlier = dot(in_pair, before)
    index = jnp.sum(in_pair * earlier, axis=0, keepdims=True)
    placed = (honest == 1) & (index < room)
    placed_earlier = jnp.sum(jnp.minimum(earlier, float(room)), axis=0, keepdims=True)
    filler_rank = iota((1, units), 1).astype(F32) - placed_earlier
    held = jnp.minimum(jnp.sum(in_pair, axis=1, keepdims=True), float(room))
    free = jnp.broadcast_to(room - held, (PAIRS, units))
    first = free
    for step in (1, 2, 4):
        first = first + jnp.concatenate([jnp.zeros((step, units), F32), first[: PAIRS - step]], axis=0)
    first = first - free
    in_gap = (filler_rank >= first) & (filler_rank < first + free)
    gap_lane = jnp.sum(
        jnp.where(in_gap, group.astype(F32) * room + held - first + filler_rank, 0.0), axis=0, keepdims=True
    )
    lane = jnp.where(placed, pair * room + index.astype(jnp.int32), gap_lane.astype(jnp.int32))
    lane = lane ^ (room * (me & 3))
    place = jnp.where(iota((units, units), 0) == lane, 1.0, 0.0).astype(BF16)
    place_ref[...] = place

    flat = jnp.concatenate([chosen_ref[n : n + 1, :] for n in range(NODES)], axis=1)
    hot = jnp.where(iota((covars, NODES * slots), 0) == flat, 1.0, 0.0)
    per_node = dot(hot, codes_ref[...].astype(F32), (((0,), (0,)), ((), ())))
    picked = jnp.zeros((slots, units), F32)
    for n in range(NODES):
        picked = picked + jnp.where(node == n, per_node[n * slots : (n + 1) * slots], 0.0)
    for j in range(owners):
        scratch[j, 0:per_owner] = picked[j * per_owner : (j + 1) * per_owner]
    ordered = [scratch[me ^ j ^ k][0:per_owner] for j in range(owners // 2) for k in (0, owners // 2)]

    keys = [node.astype(F32), arm.astype(F32), honest.astype(F32), jnp.zeros((1, units), F32)]
    wide = jnp.concatenate([outcome_ref[...].astype(F32), *keys, *ordered, jnp.zeros((4, units), F32)], axis=0)
    mine_ref[...] = dot(wide, place, NT)


def join_kernel(per_owner, place_ref, mine_ref, other_ref, own_ref, away_ref):
    weeks = other_ref.shape[0]
    mine = mine_ref[...]
    tail = mine[weeks:]
    outcome, other = mine[0:weeks], dot(other_ref[...], place_ref[...], NT)
    first = (lax.axis_index("period") & 1) == 0
    both = [jnp.where(first, outcome, other), jnp.where(first, other, outcome)]
    own_ref[...] = jnp.concatenate([*both, tail], axis=0).astype(BF16)
    turned = [
        tail[at : at + per_owner]
        for pair in range(4, tail.shape[0] - 4, 2 * per_owner)
        for at in (pair + per_owner, pair)
    ]
    away_ref[...] = jnp.concatenate([*both, tail[0:4], *turned, tail[-4:]], axis=0).astype(BF16)


def gain_kernel(layout, per_owner, periods, *refs):
    n_in = len(layout)
    blocks = refs[:n_in]
    gain_ref, effect_ref, outs, keys, sums = refs[n_in:]
    weeks, depth, key_rows = outs.shape[1], outs.shape[2], keys.shape[1]
    me, period = lax.axis_index("row"), lax.axis_index("period")
    where_of = {k: (ref, at) for ref, ids in zip(blocks, layout) for at, k in enumerate(ids)}
    n_blocks = len(where_of)
    quarter = lax.shift_right_logical(iota((8, LANES), 1), 5) ^ (me & 3)
    masks = [quarter == t for t in range(4)]
    one, zero = jnp.ones((), BF16), jnp.zeros((), BF16)

    share = BINS // periods
    row = iota((BINS // 2, depth), 0)
    index, within = row // share, row % share
    odd = period ^ index
    for shift in (2, 1):
        odd = odd ^ lax.shift_right_logical(odd, shift)
    bins_up = ((2 * index + (odd & 1)) * share + within + 1).astype(F32).astype(BF16)

    def loaded(k, half):
        ref, at = where_of[k]
        return ref[at, 0 : weeks + key_rows, half * LANES : (half + 1) * LANES].astype(F32)

    def week_rows(g, out, key):
        node, arm, honest = key[0:1], key[1:2], key[2:3]
        mine, counts = [], []
        for m in range(2):
            of_node = (node == (2 * g + m).astype(F32)) & (honest == 1.0)
            arms = [jnp.where(of_node & (arm == a), 1.0, 0.0) for a in (1.0, 0.0)]
            counts += [jnp.broadcast_to(here, (8, here.shape[1])) for here in arms]
            mine += [out[w : w + 8] * here for w in range(0, weeks, 8) for here in arms]
        return jnp.concatenate(counts + mine, axis=0)

    def step_rows(key, tile):
        steps = []
        for s in (2 * tile, 2 * tile + 1):
            pick = jnp.broadcast_to(key[4 + s : 5 + s], (16, key.shape[1])).astype(BF16)
            pick = jnp.concatenate([pick] * (BINS // 32), axis=0)
            steps.append(jnp.maximum(jnp.minimum(bins_up - pick, one), zero))
        return jnp.concatenate(steps, axis=0)

    def pair_gains(left, total):
        gains = []
        for m in range(2):
            base, count = 32 + 2 * m * weeks, 16 * m
            lt, lc = left[count : count + 8], left[count + 8 : count + 16]
            rt, rc = total[count : count + 8] - lt, total[count + 8 : count + 16] - lc
            it, ic = 1.0 / (rt + 1.0), 1.0 / (rc + 1.0)
            at, ac = 1.0 / (lt + 1.0) + it, 1.0 / (lc + 1.0) + ic
            spread = None
            for w in range(base, base + 2 * weeks, 16):
                treated, control = slice(w, w + 8), slice(w + 8, w + 16)
                gap = (left[treated] * at - total[treated] * it) - (left[control] * ac - total[control] * ic)
                spread = gap * gap if spread is None else spread + gap * gap
            cl, cr = lt + lc, rt + rc
            balance = cl * cr / ((cl + cr + 1.0) * (cl + cr + 1.0))
            gains.append(jnp.sum(balance * spread, axis=0, keepdims=True))
        return gains

    def totals(mine):
        return jnp.broadcast_to(jnp.sum(mine, axis=1, keepdims=True), (mine.shape[0], BINS // 2))

    def store(tile, nodes, left, total):
        for h in range(2):
            for m, gain in enumerate(pair_gains(left[:, h * BINS // 2 : (h + 1) * BINS // 2], total)):
                gain_ref[2 * tile + h, nodes[m]] = gain

    strays = jnp.zeros((1, depth), F32)
    est = jnp.zeros((2 * NODES, weeks // 2), F32)
    est_units = jnp.zeros((2 * NODES, depth), F32)
    for half in range(2):
        held = [loaded(k, half) for k in range(n_blocks)]
        for g in range(half * 4, half * 4 + 4):
            parts = []
            for first in range(0, n_blocks, 4):
                part = held[first]
                for k in range(first + 1, first + 4):
                    mask = jnp.concatenate([masks[(g ^ k) & 3]] * (part.shape[0] // 8), axis=0)
                    part = jnp.where(mask, held[k], part)
                parts.append(part)
            block = jnp.concatenate(parts, axis=1)
            out, key = block[0:weeks], block[weeks:]
            outs[g] = out
            keys[g] = key
            node, arm, honest = key[0:1], key[1:2], key[2:3]
            strays = strays + jnp.where((honest == 1.0) & ((node < 2.0 * g) | (node > 2.0 * g + 1.0)), 1.0, 0.0)
            kept = jnp.where(honest == 0.0, node, -1.0)
            kept_hot = kept == iota((NODES, depth), 0).astype(F32)
            hot = jnp.concatenate(
                [jnp.where(kept_hot & (arm == a), 1.0, 0.0) for a in (1.0, 0.0)], axis=0
            )
            est = est + dot(hot, jnp.where((period & 1) == 0, out[: weeks // 2], out[weeks // 2 :]), NT)
            est_units = est_units + hot
            mine = week_rows(jnp.int32(g), out, key)
            total = totals(mine)
            lefts = [dot(mine, step_rows(key, tile), NT) for tile in range(per_owner)]
            for tile, left in enumerate(lefts):
                store(tile, [slice(2 * g + m, 2 * g + m + 1) for m in range(2)], left, total)

    units = jnp.sum(est_units, axis=1, keepdims=True)
    effect_ref[...] = est / (units + 1.0)

    @pl.when(jnp.sum(strays) > 0.0)
    def _():
        def over_pairs(g, carry):
            for tile in range(per_owner):
                sums[...] = jnp.zeros_like(sums)

                def over_lanes(other, total):
                    mine = week_rows(g, outs[other], keys[other])
                    sums[...] += dot(mine, step_rows(keys[other], tile), NT)
                    return total + totals(mine)

                total = lax.fori_loop(0, PAIRS, over_lanes, jnp.zeros((sums.shape[0], BINS // 2), F32))
                store(tile, [pl.ds(2 * g + m, 1) for m in range(2)], sums[...], total)
            return carry

        lax.fori_loop(0, PAIRS, over_pairs, 0)


def shards(codes, node, chosen, arm, honest, outcome):
    units, weeks = outcome.shape
    slots = chosen.shape[1]
    owners, periods = lax.axis_size("row"), lax.axis_size("period")
    per_owner = slots // owners
    vmem = pl.BlockSpec(memory_space=pltpu.VMEM)

    def swap(x, axis, bit):
        return lax.ppermute(x, axis, [(i, i ^ bit) for i in range(lax.axis_size(axis))])

    def cross(x, bit):
        return swap(x, ("row", "period"), bit * periods | 1)

    inputs = (codes.T, node.reshape(1, units), arm.reshape(1, units), honest.reshape(1, units), chosen, outcome.T)
    other = swap(outcome.T, "period", 1)
    place, mine = pl.pallas_call(
        functools.partial(place_kernel, owners),
        out_shape=(
            jax.ShapeDtypeStruct((units, units), BF16),
            jax.ShapeDtypeStruct((weeks + 8 + slots, units), F32),
        ),
        in_specs=[vmem] * 6,
        out_specs=(vmem, vmem),
        compiler_params=pltpu.CompilerParams(vmem_limit_bytes=8 * 1024 * 1024),
        scratch_shapes=[pltpu.VMEM((owners, -(-per_owner // 8) * 8, units), F32)],
    )(*(pltpu.with_memory_space_constraint(x, pltpu.HBM) for x in inputs))
    packed = jax.ShapeDtypeStruct((2 * weeks + 8 + slots, units), BF16)
    own, away = pl.pallas_call(
        functools.partial(join_kernel, per_owner),
        out_shape=(packed, packed),
        in_specs=[vmem] * 3,
        out_specs=(vmem, vmem),
        compiler_params=pltpu.CompilerParams(vmem_limit_bytes=4 * 1024 * 1024),
    )(place, mine, other)

    bins_at, width = 2 * weeks + 4, 2 * per_owner
    key_rows = -(-(4 + width) // 8) * 8

    def part(x, first, last, more):
        return jnp.concatenate([x[:, :bins_at], x[:, bins_at + first * width : bins_at + last * width + more]], axis=1)

    half = owners // 2
    held = [(own[None], [0]), (cross(away, half)[None], [half])]
    groups = half
    while groups > 4:
        groups //= 2
        ids = [k for _, some in held for k in some]
        whole = jnp.concatenate([x for x, _ in held], axis=0)
        came = cross(part(whole, groups, 2 * groups, 4), groups)
        held = [(part(whole, 0, groups, 4), ids), (came, [k ^ groups for k in ids])]
    layout = [some for _, some in held]
    blocks = [x for x, _ in held]
    for (x, some), order in zip(held, ((1, 3, 2), (1, 3, 2))):
        for k in order:
            blocks.append(cross(part(x, k, k + 1, key_rows - 4 - width), k))
            layout.append([i ^ k for i in some])

    depth = owners * units // PAIRS
    gain, effect = pl.pallas_call(
        functools.partial(gain_kernel, layout, per_owner, periods),
        out_shape=(
            jax.ShapeDtypeStruct((2 * per_owner, NODES, BINS // 2), F32),
            jax.ShapeDtypeStruct((2 * NODES, weeks), F32),
        ),
        in_specs=[vmem] * len(blocks),
        out_specs=(vmem, vmem),
        scratch_shapes=[
            pltpu.VMEM((PAIRS, 2 * weeks, depth), F32),
            pltpu.VMEM((PAIRS, key_rows, depth), F32),
            pltpu.VMEM((8 * weeks + 32, BINS), F32),
        ],
        compiler_params=pltpu.CompilerParams(vmem_limit_bytes=16 * 1024 * 1024),
    )(*blocks)

    bit = 2
    while bit < periods:
        gain = gain + swap(gain, "period", bit | 1)
        bit *= 2
    share = BINS // periods
    gains = lax.dynamic_slice_in_dim(gain[:per_owner], (lax.axis_index("period") >> 1) * share, share, 2)
    best = jnp.max(gain, axis=(0, 2))
    best = jnp.maximum(best, swap(best, "period", 1))
    bit = 1
    while bit < half:
        best = jnp.maximum(best, cross(best, bit))
        bit *= 2
    return gains, best, effect[:NODES] - effect[NODES:]


def solution(mesh):
    in_specs = (P("row", None), P("row"), P(), P("row"), P("row"), P("row", "period"))
    out_specs = (P("row", None, "period"), P(), P(None, "period"))
    return jax.shard_map(shards, mesh=mesh, in_specs=in_specs, out_specs=out_specs, check_vma=False)
```

```python
import functools

import jax
import jax.numpy as jnp
from jax import lax
from jax.experimental import pallas as pl
from jax.experimental.pallas import tpu as pltpu
from jax.sharding import PartitionSpec as P

NODES = 16
BINS = 256
LANES = 128
PAIRS = NODES // 2
BF16 = jnp.bfloat16
F32 = jnp.float32
NT = (((1,), (1,)), ((), ()))


def iota(shape, axis):
    return lax.broadcasted_iota(jnp.int32, shape, axis)


def dot(a, b, dims=(((1,), (0,)), ((), ()))):
    return lax.dot_general(a.astype(BF16), b.astype(BF16), dims, preferred_element_type=F32)


def place_kernel(owners, codes_ref, node_ref, arm_ref, honest_ref, chosen_ref, outcome_ref, place_ref, mine_ref, scratch):
    covars, units = codes_ref.shape
    slots, weeks = chosen_ref.shape[1], outcome_ref.shape[0]
    per_owner = slots // owners
    room = units // PAIRS
    me = lax.axis_index("row")
    node, arm, honest = node_ref[...], arm_ref[...], honest_ref[...]

    before = (iota((units, units), 0) < iota((units, units), 1)).astype(BF16)
    pair = lax.shift_right_logical(node, 1)
    group = iota((PAIRS, units), 0)
    in_pair = ((group == pair) & (honest == 1)).astype(F32)
    earlier = dot(in_pair, before)
    index = jnp.sum(in_pair * earlier, axis=0, keepdims=True)
    placed = (honest == 1) & (index < room)
    placed_earlier = jnp.sum(jnp.minimum(earlier, float(room)), axis=0, keepdims=True)
    filler_rank = iota((1, units), 1).astype(F32) - placed_earlier
    held = jnp.minimum(jnp.sum(in_pair, axis=1, keepdims=True), float(room))
    free = jnp.broadcast_to(room - held, (PAIRS, units))
    first = free
    for step in (1, 2, 4):
        first = first + jnp.concatenate([jnp.zeros((step, units), F32), first[: PAIRS - step]], axis=0)
    first = first - free
    in_gap = (filler_rank >= first) & (filler_rank < first + free)
    gap_lane = jnp.sum(
        jnp.where(in_gap, group.astype(F32) * room + held - first + filler_rank, 0.0), axis=0, keepdims=True
    )
    lane = jnp.where(placed, pair * room + index.astype(jnp.int32), gap_lane.astype(jnp.int32))
    lane = lane ^ (room * (me & 3))
    place = jnp.where(iota((units, units), 0) == lane, 1.0, 0.0).astype(BF16)
    place_ref[...] = place

    flat = jnp.concatenate([chosen_ref[n : n + 1, :] for n in range(NODES)], axis=1)
    hot = jnp.where(iota((covars, NODES * slots), 0) == flat, 1.0, 0.0)
    per_node = dot(hot, codes_ref[...].astype(F32), (((0,), (0,)), ((), ())))
    picked = jnp.zeros((slots, units), F32)
    for n in range(NODES):
        picked = picked + jnp.where(node == n, per_node[n * slots : (n + 1) * slots], 0.0)
    for j in range(owners):
        scratch[j, 0:per_owner] = picked[j * per_owner : (j + 1) * per_owner]
    ordered = [scratch[me ^ j ^ k][0:per_owner] for j in range(owners // 2) for k in (0, owners // 2)]

    keys = [node.astype(F32), arm.astype(F32), honest.astype(F32), jnp.zeros((1, units), F32)]
    wide = jnp.concatenate([outcome_ref[...].astype(F32), *keys, *ordered, jnp.zeros((4, units), F32)], axis=0)
    mine_ref[...] = dot(wide, place, NT)


def join_kernel(per_owner, place_ref, mine_ref, other_ref, own_ref, away_ref):
    weeks = other_ref.shape[0]
    mine = mine_ref[...]
    tail = mine[weeks:]
    outcome, other = mine[0:weeks], dot(other_ref[...], place_ref[...], NT)
    first = (lax.axis_index("period") & 1) == 0
    both = [jnp.where(first, outcome, other), jnp.where(first, other, outcome)]
    own_ref[...] = jnp.concatenate([*both, tail], axis=0).astype(BF16)
    turned = [
        tail[at : at + per_owner]
        for pair in range(4, tail.shape[0] - 4, 2 * per_owner)
        for at in (pair + per_owner, pair)
    ]
    away_ref[...] = jnp.concatenate([*both, tail[0:4], *turned, tail[-4:]], axis=0).astype(BF16)


def gain_kernel(layout, per_owner, periods, *refs):
    n_in = len(layout)
    blocks = refs[:n_in]
    gain_ref, effect_ref, outs, keys, sums = refs[n_in:]
    weeks, depth, key_rows = outs.shape[1], outs.shape[2], keys.shape[1]
    me, period = lax.axis_index("row"), lax.axis_index("period")
    where_of = {k: (ref, at) for ref, ids in zip(blocks, layout) for at, k in enumerate(ids)}
    n_blocks = len(where_of)
    quarter = lax.shift_right_logical(iota((8, LANES), 1), 5) ^ (me & 3)
    masks = [quarter == t for t in range(4)]
    one, zero = jnp.ones((), BF16), jnp.zeros((), BF16)

    share = BINS // periods
    row = iota((BINS // 2, depth), 0)
    index, within = row // share, row % share
    odd = period ^ index
    for shift in (2, 1):
        odd = odd ^ lax.shift_right_logical(odd, shift)
    bins_up = ((2 * index + (odd & 1)) * share + within + 1).astype(F32).astype(BF16)

    def loaded(k, half):
        ref, at = where_of[k]
        return ref[at, 0 : weeks + key_rows, half * LANES : (half + 1) * LANES].astype(F32)

    def week_rows(g, out, key):
        node, arm, honest = key[0:1], key[1:2], key[2:3]
        mine, counts = [], []
        for m in range(2):
            of_node = (node == (2 * g + m).astype(F32)) & (honest == 1.0)
            arms = [jnp.where(of_node & (arm == a), 1.0, 0.0) for a in (1.0, 0.0)]
            counts += [jnp.broadcast_to(here, (8, here.shape[1])) for here in arms]
            mine += [out[w : w + 8] * here for w in range(0, weeks, 8) for here in arms]
        return jnp.concatenate(counts + mine, axis=0)

    def step_rows(key, tile):
        steps = []
        for s in (2 * tile, 2 * tile + 1):
            pick = jnp.broadcast_to(key[4 + s : 5 + s], (16, key.shape[1])).astype(BF16)
            pick = jnp.concatenate([pick] * (BINS // 32), axis=0)
            steps.append(jnp.maximum(jnp.minimum(bins_up - pick, one), zero))
        return jnp.concatenate(steps, axis=0)

    def pair_gains(left, total):
        gains = []
        for m in range(2):
            base, count = 32 + 2 * m * weeks, 16 * m
            lt, lc = left[count : count + 8], left[count + 8 : count + 16]
            rt, rc = total[count : count + 8] - lt, total[count + 8 : count + 16] - lc
            it, ic = 1.0 / (rt + 1.0), 1.0 / (rc + 1.0)
            at, ac = 1.0 / (lt + 1.0) + it, 1.0 / (lc + 1.0) + ic
            spread = None
            for w in range(base, base + 2 * weeks, 16):
                treated, control = slice(w, w + 8), slice(w + 8, w + 16)
                gap = (left[treated] * at - total[treated] * it) - (left[control] * ac - total[control] * ic)
                spread = gap * gap if spread is None else spread + gap * gap
            cl, cr = lt + lc, rt + rc
            balance = cl * cr / ((cl + cr + 1.0) * (cl + cr + 1.0))
            gains.append(jnp.sum(balance * spread, axis=0, keepdims=True))
        return gains

    def totals(mine):
        return jnp.broadcast_to(jnp.sum(mine, axis=1, keepdims=True), (mine.shape[0], BINS // 2))

    def store(tile, nodes, left, total):
        for h in range(2):
            for m, gain in enumerate(pair_gains(left[:, h * BINS // 2 : (h + 1) * BINS // 2], total)):
                gain_ref[2 * tile + h, nodes[m]] = gain

    strays = jnp.zeros((1, depth), F32)
    est = jnp.zeros((2 * NODES, weeks // 2), F32)
    est_units = jnp.zeros((2 * NODES, depth), F32)
    for half in range(2):
        held = [loaded(k, half) for k in range(n_blocks)]
        for g in range(half * 4, half * 4 + 4):
            parts = []
            for first in range(0, n_blocks, 4):
                part = held[first]
                for k in range(first + 1, first + 4):
                    mask = jnp.concatenate([masks[(g ^ k) & 3]] * (part.shape[0] // 8), axis=0)
                    part = jnp.where(mask, held[k], part)
                parts.append(part)
            block = jnp.concatenate(parts, axis=1)
            out, key = block[0:weeks], block[weeks:]
            outs[g] = out
            keys[g] = key
            node, arm, honest = key[0:1], key[1:2], key[2:3]
            strays = strays + jnp.where((honest == 1.0) & ((node < 2.0 * g) | (node > 2.0 * g + 1.0)), 1.0, 0.0)
            kept = jnp.where(honest == 0.0, node, -1.0)
            kept_hot = kept == iota((NODES, depth), 0).astype(F32)
            hot = jnp.concatenate(
                [jnp.where(kept_hot & (arm == a), 1.0, 0.0) for a in (1.0, 0.0)], axis=0
            )
            est = est + dot(hot, jnp.where((period & 1) == 0, out[: weeks // 2], out[weeks // 2 :]), NT)
            est_units = est_units + hot
            mine = week_rows(jnp.int32(g), out, key)
            total = totals(mine)
            lefts = [dot(mine, step_rows(key, tile), NT) for tile in range(per_owner)]
            for tile, left in enumerate(lefts):
                store(tile, [slice(2 * g + m, 2 * g + m + 1) for m in range(2)], left, total)

    units = jnp.sum(est_units, axis=1, keepdims=True)
    effect_ref[...] = est / (units + 1.0)

    @pl.when(jnp.sum(strays) > 0.0)
    def _():
        def over_pairs(g, carry):
            for tile in range(per_owner):
                sums[...] = jnp.zeros_like(sums)

                def over_lanes(other, total):
                    mine = week_rows(g, outs[other], keys[other])
                    sums[...] += dot(mine, step_rows(keys[other], tile), NT)
                    return total + totals(mine)

                total = lax.fori_loop(0, PAIRS, over_lanes, jnp.zeros((sums.shape[0], BINS // 2), F32))
                store(tile, [pl.ds(2 * g + m, 1) for m in range(2)], sums[...], total)
            return carry

        lax.fori_loop(0, PAIRS, over_pairs, 0)


def shards(codes, node, chosen, arm, honest, outcome):
    units, weeks = outcome.shape
    slots = chosen.shape[1]
    owners, periods = lax.axis_size("row"), lax.axis_size("period")
    per_owner = slots // owners
    vmem = pl.BlockSpec(memory_space=pltpu.VMEM)

    def swap(x, axis, bit):
        return lax.ppermute(x, axis, [(i, i ^ bit) for i in range(lax.axis_size(axis))])

    def cross(x, bit):
        return swap(x, ("row", "period"), bit * periods | 1)

    inputs = (codes.T, node.reshape(1, units), arm.reshape(1, units), honest.reshape(1, units), chosen, outcome.T)
    other = swap(outcome.T, "period", 1)
    place, mine = pl.pallas_call(
        functools.partial(place_kernel, owners),
        out_shape=(
            jax.ShapeDtypeStruct((units, units), BF16),
            jax.ShapeDtypeStruct((weeks + 8 + slots, units), F32),
        ),
        in_specs=[vmem] * 6,
        out_specs=(vmem, vmem),
        compiler_params=pltpu.CompilerParams(vmem_limit_bytes=8 * 1024 * 1024),
        scratch_shapes=[pltpu.VMEM((owners, -(-per_owner // 8) * 8, units), F32)],
    )(*(pltpu.with_memory_space_constraint(x, pltpu.HBM) for x in inputs))
    packed = jax.ShapeDtypeStruct((2 * weeks + 8 + slots, units), BF16)
    own, away = pl.pallas_call(
        functools.partial(join_kernel, per_owner),
        out_shape=(packed, packed),
        in_specs=[vmem] * 3,
        out_specs=(vmem, vmem),
        compiler_params=pltpu.CompilerParams(vmem_limit_bytes=4 * 1024 * 1024),
    )(place, mine, other)

    bins_at, width = 2 * weeks + 4, 2 * per_owner
    key_rows = -(-(4 + width) // 8) * 8

    def part(x, first, last, more):
        return jnp.concatenate([x[:, :bins_at], x[:, bins_at + first * width : bins_at + last * width + more]], axis=1)

    half = owners // 2
    held = [(own[None], [0]), (cross(away, half)[None], [half])]
    groups = half
    while groups > 4:
        groups //= 2
        ids = [k for _, some in held for k in some]
        whole = jnp.concatenate([x for x, _ in held], axis=0)
        came = cross(part(whole, groups, 2 * groups, 4), groups)
        held = [(part(whole, 0, groups, 4), ids), (came, [k ^ groups for k in ids])]
    layout = [some for _, some in held]
    blocks = [x for x, _ in held]
    def sent(x, k):
        return part(x, k, k + 1, key_rows - 4 - width)

    (kept, some), (came, others) = held
    for k in (1, 2):
        blocks.append(cross(sent(kept, k), k))
        layout.append([i ^ k for i in some])
    for k in (3, 2, 1):
        if k in (1, 2):
            blocks.append(cross(sent(came, k), k))
            layout.append([i ^ k for i in others])
        else:
            blocks.append(cross(jnp.concatenate([sent(kept, k), sent(came, k)], axis=0), k))
            layout.append([i ^ k for i in some + others])

    depth = owners * units // PAIRS
    gain, effect = pl.pallas_call(
        functools.partial(gain_kernel, layout, per_owner, periods),
        out_shape=(
            jax.ShapeDtypeStruct((2 * per_owner, NODES, BINS // 2), F32),
            jax.ShapeDtypeStruct((2 * NODES, weeks), F32),
        ),
        in_specs=[vmem] * len(blocks),
        out_specs=(vmem, vmem),
        scratch_shapes=[
            pltpu.VMEM((PAIRS, 2 * weeks, depth), F32),
            pltpu.VMEM((PAIRS, key_rows, depth), F32),
            pltpu.VMEM((8 * weeks + 32, BINS), F32),
        ],
        compiler_params=pltpu.CompilerParams(vmem_limit_bytes=16 * 1024 * 1024),
    )(*blocks)

    bit = 2
    while bit < periods:
        gain = gain + swap(gain, "period", bit | 1)
        bit *= 2
    share = BINS // periods
    gains = lax.dynamic_slice_in_dim(gain[:per_owner], (lax.axis_index("period") >> 1) * share, share, 2)
    best = jnp.max(gain, axis=(0, 2))
    bit = half // 2
    while bit:
        best = jnp.maximum(best, cross(best, bit))
        bit //= 2
    best = jnp.maximum(best, swap(best, "period", 1))
    return gains, best, effect[:NODES] - effect[NODES:]


def solution(mesh):
    in_specs = (P("row", None), P("row"), P(), P("row"), P("row"), P("row", "period"))
    out_specs = (P("row", None, "period"), P(), P(None, "period"))
    return jax.shard_map(shards, mesh=mesh, in_specs=in_specs, out_specs=out_specs, check_vma=False)
```
